32 devices in a mesh: grp: 2 (over core), seg: 16 (over z, y, x).
Axes of the slice: x: 2, y: 2, z: 4, core: 2. Of those that a mesh axis runs over, the one named last changes fastest.
Arguments:
- frames_in: bfloat16 [2048, 20, 512], P(('grp', 'seg')), may hold values from -6 to 6
- memory: bfloat16 [2048, 512], P(('grp', 'seg')), may hold values from -6 to 6
- counts: int32 [2, 48], P('grp'), may hold values from 1 to 32, 1024 in all within a row
- query_weight: bfloat16 [512, 512], replicated, may hold values from -0.25 to 0.25
- key_weight: bfloat16 [512, 512], replicated, may hold values from -0.25 to 0.25
- value_weight: bfloat16 [512, 512], replicated, may hold values from -0.25 to 0.25
- out_weight: bfloat16 [512, 512], replicated, may hold values from -1 to 1
- up_weight: bfloat16 [512, 2048], replicated, may hold values from -0.25 to 0.25
- down_weight: bfloat16 [2048, 512], replicated, may hold values from -0.125 to 0.125
- input_gain: float32 [512], replicated, may hold values from 0.1 to 1.9
- middle_gain: float32 [512], replicated, may hold values from 0.1 to 1.9
- output_gain: float32 [512], replicated, may hold values from 0.1 to 1.9
- out_grad: bfloat16 [2048, 20, 512], P(('grp', 'seg')), may hold values from -6 to 6
- memory_grad: bfloat16 [2048, 512], P(('grp', 'seg')), may hold values from -6 to 6
Outputs:
- result_frames: bfloat16 [2048, 20, 512], P(('grp', 'seg'))
- memory_out: bfloat16 [2048, 512], P(('grp', 'seg'))
- grad_frames: float32 [2048, 20, 512], P(('grp', 'seg'))
- grad_memory: bfloat16 [2048, 512], P(('grp', 'seg'))
- grad_query: float32 [512, 512], replicated
- grad_key: float32 [512, 512], replicated
- grad_value: float32 [512, 512], replicated
- grad_out: float32 [512, 512], replicated
- grad_up: float32 [512, 2048], replicated
- grad_down: float32 [2048, 512], replicated
- grad_input_gain: float32 [512], replicated
- grad_middle_gain: float32 [512], replicated
- grad_output_gain: float32 [512], replicated
The draws below stay inside these ranges and needn't reach their ends.
Inputs may be any that keep to these rules, and one draw needn't show every extreme that they name: In each group the 48 counts sum to 1024, and the largest is exactly 32.
All inputs are finite; a program needn't handle non-finite values.
Results may differ from the reference program's by a relative error of at most 0.015.
Values may be sent and summed in bfloat16 or wider, within the bound.
No kernel may reach another device: no remote copies, remote signals or barrier semaphores. Data moves between devices by JAX's collectives and lax.ppermute only.
A program may use at most 320 MiB of HBM per device.

```python
import math
import jax
import jax.numpy as jnp
import numpy as np
from jax import lax

D = 512
HEADS = 8
HDIM = 64
FF = 2048
SEGLEN = 16
RIGHT = 4
LEFT = 30
MEMS = 4
SLOTS = 64
FRAMES = 20
GSEG = 1024
SEGS = 2048
UTTS = 48
N_GRP = 2
N_SEG = 16


def steps_of(key, dims, cuts, low, largest):
    factor_of = 1.0
    for dim, parts in cuts:
        steps = jax.random.uniform(jax.random.fold_in(jax.random.fold_in(key, 6), dim), (parts,), jnp.float32, low / len(cuts), largest / len(cuts))
        factor_of = factor_of * jnp.repeat(jnp.exp(steps), dims[dim] // parts).reshape((-1,) + (1,) * (len(dims) - 1 - dim))
    return factor_of


def split_up(amount, total, reach, slope):
    loads = [(1 << 20) // math.isqrt(rank ** slope) + 1 for rank in range(2, amount + 1)]
    rest, given = total - reach - (amount - 1), [1] * (amount - 1)
    while rest > 0:
        candidates = [i for i in range(amount - 1) if given[i] < reach]
        whole, left = sum([loads[i] for i in candidates]), rest
        for i in candidates:
            more = min(reach - given[i], max(1, left * loads[i] // whole), rest)
            given[i] = given[i] + more
            rest = rest - more
    return np.array([reach] + given)


def ragged(stream_key, number_of, total, most, lean):
    if number_of == 2:
        one = jax.random.randint(stream_key, (), max(1, total - most), min(most, total - 1) + 1)
        return jnp.stack([one, total - one])
    tallies = jnp.asarray(split_up(number_of, total, most, lean), jnp.int32)
    couples = (number_of - 1) // 2
    giver, sink = tallies[1:1 + 2 * couples:2], tallies[2:2 + 2 * couples:2]
    room = jnp.minimum(giver - 1, most - sink)
    passed = jax.random.randint(jax.random.fold_in(stream_key, 1), (couples,), 0, 1 << 20) % (room + 1)
    tallies = tallies.at[1:1 + 2 * couples:2].set(giver - passed).at[2:2 + 2 * couples:2].set(sink + passed)
    return tallies[jax.random.permutation(jax.random.fold_in(stream_key, 2), number_of)]


def noise(rng, extent, deviation, most, split=(), kind=jnp.bfloat16):
    values = deviation * jax.random.normal(rng, extent, jnp.float32)
    if split:
        values = values * steps_of(rng, extent, split, -0.22, 0.18)
    return jnp.clip(values, -most, most).astype(kind)


def setup_inputs(seed: int = 0) -> dict:
    seeds = jax.random.split(jax.random.key(seed), 15)
    frames_in = noise(seeds[0], (SEGS, FRAMES, D), 1.0, 6.0, ((0, 32),))
    memory = noise(seeds[1], (SEGS, D), 1.0, 6.0, ((0, 32),))
    counts = jax.vmap(lambda own: ragged(own, UTTS, GSEG, 2 * N_SEG, 2))(jax.random.split(seeds[2], N_GRP)).reshape((N_GRP, UTTS)).astype(jnp.int32)
    query_weight = noise(seeds[3], (D, D), D ** -0.5, 0.25)
    key_weight = noise(seeds[4], (D, D), D ** -0.5, 0.25)
    value_weight = noise(seeds[5], (D, D), D ** -0.5, 0.25)
    out_weight = noise(seeds[6], (D, D), (D // 16) ** -0.5, 1.0)
    up_weight = noise(seeds[7], (D, FF), D ** -0.5, 0.25)
    down_weight = noise(seeds[8], (FF, D), FF ** -0.5, 0.125)
    input_gain = jnp.clip(1.0 + 0.18 * jax.random.normal(seeds[9], (D,), jnp.float32), 0.1, 1.9)
    middle_gain = jnp.clip(1.0 + 0.18 * jax.random.normal(seeds[10], (D,), jnp.float32), 0.1, 1.9)
    output_gain = jnp.clip(1.0 + 0.18 * jax.random.normal(seeds[11], (D,), jnp.float32), 0.1, 1.9)
    out_grad = noise(seeds[12], (SEGS, FRAMES, D), 1.0, 6.0, ((0, 32),))
    memory_grad = noise(seeds[13], (SEGS, D), 1.0, 6.0, ((0, 32),))
    return dict(frames_in=frames_in, memory=memory, counts=counts, query_weight=query_weight, key_weight=key_weight, value_weight=value_weight, out_weight=out_weight, up_weight=up_weight, down_weight=down_weight, input_gain=input_gain, middle_gain=middle_gain, output_gain=output_gain, out_grad=out_grad, memory_grad=memory_grad)


@jax.custom_vjp
def low(v):
    return lax.optimization_barrier(v.astype(jnp.bfloat16)).astype(jnp.float32)

@jax.custom_vjp
def low_back(v):
    return v

def low_keep(v):
    return (low(v), None)

def low_pass(kept, grad):
    return (grad,)

def back_keep(v):
    return (v, None)

def back_low(kept, grad):
    return (low(grad),)
low.defvjp(low_keep, low_pass)
low_back.defvjp(back_keep, back_low)
EPSILON = 1e-05
MASKED_SCORE = -1e+30

def norm_rows(values, norm_gain):
    centered = values - lax.optimization_barrier(jnp.mean(values, axis=-1, keepdims=True))
    spread = lax.optimization_barrier(jnp.mean(centered * centered, axis=-1, keepdims=True))
    return centered * lax.rsqrt(spread + EPSILON) * norm_gain

def product(operand, weight):
    return jnp.einsum('...i,ij->...j', operand, weight, precision=lax.Precision.HIGHEST)

def key_mask(position):
    columns = jnp.arange(MEMS + LEFT + SEGLEN + RIGHT, dtype=jnp.int32)
    needed = jnp.where(columns < MEMS, MEMS - columns, jnp.where(columns < MEMS + LEFT - SEGLEN, 2, jnp.where(columns < MEMS + LEFT, 1, 0)))
    queries = jnp.arange(SEGLEN + RIGHT + 1, dtype=jnp.int32)
    summary_row = (queries[:, None] == SEGLEN + RIGHT) & (columns[None, :] < MEMS)
    return (position[:, None, None] >= needed[None, None, :]) & jnp.logical_not(summary_row)[None]

def segment_position(counts_row, segment):
    starts = jnp.cumsum(counts_row, dtype=jnp.int32) - counts_row
    first_segment = lax.optimization_barrier(jnp.max(jnp.where(starts[None, :] <= segment[:, None], starts[None, :], 0), axis=1))
    return (segment - first_segment).astype(jnp.int32)

def attend(queries, all_keys, all_values, allowed):
    number = queries.shape[0]
    query_heads = queries.reshape(number, SEGLEN + RIGHT + 1, HEADS, HDIM)
    key_heads = all_keys.reshape(number, -1, HEADS, HDIM)
    value_heads = all_values.reshape(number, -1, HEADS, HDIM)
    scores = low_back(jnp.einsum('bqhe,bkhe->bhqk', query_heads, key_heads, precision=lax.Precision.HIGHEST))
    scores = jnp.where(allowed[:, None], scores, MASKED_SCORE)
    soft_scores = low(jax.nn.softmax(scores, axis=-1))
    attended = jnp.einsum('bhqk,bkhe->bqhe', soft_scores, value_heads, precision=lax.Precision.HIGHEST)
    return low_back(low(attended.reshape(number, SEGLEN + RIGHT + 1, D)))

def project_step(params, inputs):
    query_weight, key_weight, value_weight = (params[0], params[1], params[2])
    input_gain = params[6]
    frames_block, memory = inputs
    normed = norm_rows(frames_block, input_gain)
    shared = low_back(low(normed))
    summary = low_back(low(lax.optimization_barrier(jnp.mean(normed[:, RIGHT:], axis=1))))
    memory_in = low_back(memory)
    query_rows = jnp.concatenate([shared, summary[:, None]], axis=1)
    key_rows = jnp.concatenate([shared, memory_in[:, None]], axis=1)
    queries = low_back(low(product(query_rows, query_weight) * 0.125))
    key_value = low_back(low(product(key_rows, jnp.concatenate([key_weight, value_weight], axis=1))))
    return (queries, key_value)

def layer_step(params, padded_pairs, inputs):
    out_weight, up_weight, down_weight = (params[3], params[4], params[5])
    middle_gain, output_gain = (params[7], params[8])
    frames_block, queries, position, start = inputs
    number = frames_block.shape[0]
    window = lax.dynamic_slice_in_dim(padded_pairs, start, number + MEMS, axis=0)
    centers = window[:, RIGHT:SEGLEN + RIGHT]
    memories = window[:, SEGLEN + RIGHT]
    own_pairs = window[MEMS:]
    older_keys = jnp.stack([memories[column:column + number] for column in range(MEMS)], axis=1)
    all_keys = jnp.concatenate([older_keys, centers[MEMS - 2:MEMS - 2 + number, 2 * SEGLEN - LEFT:], centers[MEMS - 1:MEMS - 1 + number], own_pairs[:, RIGHT:SEGLEN + RIGHT], own_pairs[:, :RIGHT]], axis=1)
    attended = attend(queries, all_keys[..., :D], all_keys[..., D:], key_mask(position))
    branch = low_back(product(attended, out_weight))
    residual = frames_block + branch[:, :SEGLEN + RIGHT]
    memory_out = low(branch[:, SEGLEN + RIGHT])
    middle = low(norm_rows(residual, middle_gain))
    hidden = low(jax.nn.gelu(low_back(product(middle, up_weight)), approximate=False))
    combined = residual + low_back(product(hidden, down_weight))
    result = norm_rows(combined, output_gain)
    return (result, memory_out)

def group_forward(params, frames_group, memory_group, position):
    block_size = 64
    blocks = frames_group.shape[0] // block_size
    frames_blocks = frames_group.reshape(blocks, block_size, SEGLEN + RIGHT, D)
    memory_blocks = memory_group.reshape(blocks, block_size, D)
    projector = jax.checkpoint(project_step)
    queries, pairs = lax.map(lambda inputs: projector(params, inputs), (frames_blocks, memory_blocks))
    flat_pairs = pairs.reshape(blocks * block_size, SEGLEN + RIGHT + 1, 2 * D)
    padded_pairs = jnp.concatenate([jnp.zeros((MEMS, SEGLEN + RIGHT + 1, 2 * D), jnp.float32), flat_pairs], axis=0)
    starts = jnp.arange(blocks, dtype=jnp.int32) * block_size
    layer = jax.checkpoint(layer_step)
    inputs = (frames_blocks, queries, position.reshape(blocks, block_size), starts)
    result, memory_out = lax.map(lambda block_inputs: layer(params, padded_pairs, block_inputs), inputs)
    return (result.reshape(-1, SEGLEN + RIGHT, D), memory_out.reshape(-1, D))

def reference(frames_in, memory, counts, query_weight, key_weight, value_weight, out_weight, up_weight, down_weight, input_gain, middle_gain, output_gain, out_grad, memory_grad):
    params = tuple((weight.astype(jnp.float32) for weight in (query_weight, key_weight, value_weight, out_weight, up_weight, down_weight, input_gain, middle_gain, output_gain)))
    group_len = N_SEG * SLOTS
    frames_all = frames_in.astype(jnp.float32).reshape(N_GRP, group_len, SEGLEN + RIGHT, D)
    memory_all = memory.astype(jnp.float32).reshape(N_GRP, group_len, D)
    cot_frames = out_grad.astype(jnp.float32).reshape(N_GRP, group_len, SEGLEN + RIGHT, D)
    cot_memory = memory_grad.astype(jnp.float32).reshape(N_GRP, group_len, D)
    results, memories_out, frame_grads, memory_grads = ([], [], [], [])
    weight_grads = jax.tree.map(jnp.zeros_like, params)
    for group_index in range(N_GRP):
        position = segment_position(counts[group_index], jnp.arange(group_len, dtype=jnp.int32))

        def forward(params_in, frames_group, memory_group):
            return group_forward(params_in, frames_group, memory_group, position)
        outputs, pullback = jax.vjp(forward, params, frames_all[group_index], memory_all[group_index])
        gradients = pullback((cot_frames[group_index], cot_memory[group_index]))
        results.append(outputs[0])
        memories_out.append(outputs[1])
        frame_grads.append(gradients[1])
        memory_grads.append(gradients[2])
        weight_grads = tuple((total_grad + part_grad for total_grad, part_grad in zip(weight_grads, gradients[0])))
    result_frames = jnp.concatenate(results, axis=0).astype(jnp.bfloat16)
    memory_out = jnp.concatenate(memories_out, axis=0).astype(jnp.bfloat16)
    grad_frames = jnp.concatenate(frame_grads, axis=0)
    grad_memory = jnp.concatenate(memory_grads, axis=0).astype(jnp.bfloat16)
    return (result_frames, memory_out, grad_frames, grad_memory, weight_grads[0], weight_grads[1], weight_grads[2], weight_grads[3], weight_grads[4], weight_grads[5], weight_grads[6], weight_grads[7], weight_grads[8])
```

```python
import functools

import jax
import jax.numpy as jnp
import numpy as np
from jax import lax
from jax.experimental import pallas as pl
from jax.experimental.pallas import tpu as pltpu
from jax.sharding import PartitionSpec as P

HEADS = 8
HDIM = 64
SEGLEN = 16
RIGHT = 4
LEFT = 30
MEMS = 4
FRAMES = RIGHT + SEGLEN

GROUP = 4
BLOCK = 16
ROWS = BLOCK * FRAMES
GROUP_ROWS = GROUP * FRAMES
GROUPS = BLOCK // GROUP
EXTRA = 8
HALO = 2 * FRAMES
WINDOW = GROUP_ROWS + HALO + 2 * MEMS
STACK = 2 * GROUP_ROWS + 2 * EXTRA
PAIRS = HEADS // 2
PAIR = 2 * HDIM

EPSILON = 1e-05
MASKED_SCORE = -1e30
FAR = 1 << 20

BF = jnp.bfloat16
F32 = jnp.float32
VMEM_LIMIT = 60 * 1024 * 1024


def dot(a, b):
    return lax.dot_general(a, b, (((1,), (0,)), ((), ())), preferred_element_type=F32)


def dot_back(a, b):
    return lax.dot_general(a, b, (((1,), (1,)), ((), ())), preferred_element_type=F32)


def dot_outer(a, b):
    return lax.dot_general(a, b, (((0,), (0,)), ((), ())), preferred_element_type=F32)


def stack_tables():
    row = np.arange(STACK)
    extra = row >= 2 * GROUP_ROWS
    inner = (row - 2 * GROUP_ROWS) % EXTRA
    segment = np.where(extra, inner % GROUP, row % GROUP_ROWS // FRAMES)
    second = np.where(extra, row >= 2 * GROUP_ROWS + EXTRA, row >= GROUP_ROWS)
    key = np.arange(WINDOW)
    is_memory = key >= WINDOW - 2 * MEMS
    key_segment = np.where(is_memory, key - (WINDOW - 2 * MEMS) - MEMS, key // FRAMES - 2)
    within = key % FRAMES
    is_right = ~is_memory & (within < RIGHT)
    behind = segment[:, None] - key_segment[None, :]
    frame_ok = np.where(
        is_right[None],
        behind == 0,
        (behind == 0)
        | (behind == 1)
        | ((behind == 2) & (within >= RIGHT + 2 * SEGLEN - LEFT)[None]),
    )
    memory_ok = (behind >= 1) & (behind <= MEMS) & ~extra[:, None]
    ok = np.where(is_memory[None], memory_ok, frame_ok)
    need = np.where(ok, behind, FAR).astype(np.int32)
    segment_of = np.broadcast_to(segment[:, None], (STACK, WINDOW)).astype(np.int32)
    lanes = np.arange(PAIR)[None, :] >= HDIM
    head = (lanes == second[:, None]).astype(np.float32)
    return need, np.ascontiguousarray(segment_of), head


def row_stats(values):
    centered = values - jnp.mean(values, axis=-1, keepdims=True)
    spread = jnp.mean(centered * centered, axis=-1, keepdims=True)
    scale = lax.rsqrt(spread + EPSILON)
    return centered * scale, scale


def norm_back(unit, scale, gain, gradient):
    gained = gradient * gain
    along = jnp.mean(gained * unit, axis=-1, keepdims=True)
    grad = scale * (gained - jnp.mean(gained, axis=-1, keepdims=True) - unit * along)
    return grad, jnp.sum(gradient * unit, axis=0, keepdims=True)


def pack_rows(source, target, count, offset=0):
    for j in range(count):
        target[offset + j * FRAMES : offset + (j + 1) * FRAMES] = source[j].astype(F32)


def project_kernel(
    frames, before, halo, memory, memory_halo, gain, query_w, key_w, value_w,
    packed, shared, summary, query, query_extra, window,
    rows, memory_rows,
):
    step = pl.program_id(0)

    @pl.when(step == 0)
    def _():
        memory_rows[0:8] = memory_halo[...].astype(F32)
        memory_rows[8:] = memory[...].astype(F32)
        pack_rows(halo, rows, 2)

    @pl.when(step > 0)
    def _():
        pack_rows(before, rows, 2)

    pack_rows(frames, rows, BLOCK, HALO)
    packed[...] = rows[HALO:].astype(BF)
    unit, _ = row_stats(rows[...])
    normed = unit * gain[...]
    rows[...] = normed
    for j in range(BLOCK):
        at = HALO + j * FRAMES
        mean = jnp.sum(rows[at + RIGHT : at + FRAMES], axis=0, keepdims=True) * (1.0 / SEGLEN)
        spot = j // GROUP * EXTRA + j % GROUP
        summary[spot : spot + 1] = mean
        summary[spot + GROUP : spot + GROUP + 1] = jnp.zeros_like(mean)
    own = rows[HALO:].astype(BF)
    shared[...] = own
    extra = summary[...].astype(BF)
    query[...] = (dot(own, query_w[...]) * 0.125).astype(BF)
    extra_query = dot(extra, query_w[...]) * 0.125
    around = memory_rows[pl.ds(pl.multiple_of(step * BLOCK, 8), BLOCK + 8)]
    for g in range(GROUPS):
        part = extra_query[g * EXTRA : (g + 1) * EXTRA]
        query_extra[2 * g * EXTRA : 2 * (g + 1) * EXTRA] = jnp.concatenate([part, part], axis=0).astype(BF)
    wide = []
    for g in range(GROUPS):
        at = g * GROUP_ROWS
        wide.append(rows[at : at + GROUP_ROWS + HALO])
        wide.append(around[MEMS + g * GROUP : MEMS + g * GROUP + 2 * MEMS])
    wide = jnp.concatenate(wide, axis=0).astype(BF)
    width = wide.shape[1]
    window[:, :width] = dot(wide, key_w[...]).astype(BF)
    window[:, width:] = dot(wide, value_w[...]).astype(BF)


def query_stack(frames, extra, head):
    return jnp.concatenate([frames, frames, extra], axis=0) * head


def unstack(stacked, low):
    frames = jnp.where(low, stacked[:GROUP_ROWS], stacked[GROUP_ROWS : 2 * GROUP_ROWS])
    at = 2 * GROUP_ROWS
    extra = jnp.where(low, stacked[at : at + EXTRA], stacked[at + EXTRA : at + 2 * EXTRA])
    return frames, extra


def low_lanes():
    return lax.broadcasted_iota(jnp.int32, (1, PAIR), 1) < HDIM


def gelu_parts(lifted):
    bell = jnp.exp(lifted * lifted * -0.5) * 0.3989422804014327
    share = 0.5 + 0.5 * lax.erf(lifted * 0.7071067811865476)
    return lifted * share, share + lifted * bell


def forward_kernel(
    position, need, segment_of, head, query, query_extra, window, packed, out_grad,
    out_w, up_w, down_w, middle_gain, output_gain,
    attended, attended_extra, soft, residual_out, slope, grad_combined_out, result, memory_out, grad_down, grad_gain,
    rows, down_sum, hidden, memory_rows,
):
    step = pl.program_id(0)
    steps = pl.num_programs(0)
    width = packed.shape[1]
    low = low_lanes()
    head_mask = head[...]
    for g in range(GROUPS):
        first = step * BLOCK + g * GROUP
        where_row = segment_of[...]
        at_row = jnp.where(
            where_row < 2,
            jnp.where(where_row == 0, position[first], position[first + 1]),
            jnp.where(where_row == 2, position[first + 2], position[first + 3]),
        )
        bias = jnp.where(at_row >= need[...], 0.0, MASKED_SCORE)
        for p in range(PAIRS):
            lanes = slice(p * PAIR, (p + 1) * PAIR)
            value_lanes = slice(width + p * PAIR, width + (p + 1) * PAIR)
            keys = window[g * WINDOW : (g + 1) * WINDOW, lanes]
            values = window[g * WINDOW : (g + 1) * WINDOW, value_lanes]
            stack = query_stack(
                query[g * GROUP_ROWS : (g + 1) * GROUP_ROWS, lanes],
                query_extra[2 * g * EXTRA : 2 * (g + 1) * EXTRA, lanes],
                head_mask,
            )
            scores = dot_back(stack, keys) + bias
            powers = jnp.exp(scores - jnp.max(scores, axis=-1, keepdims=True))
            soft_low = (powers / jnp.sum(powers, axis=-1, keepdims=True)).astype(BF)
            at = (g * PAIRS + p) * STACK
            soft[at : at + STACK] = soft_low
            frames, extra = unstack(dot(soft_low, values), low)
            attended[g * GROUP_ROWS : (g + 1) * GROUP_ROWS, lanes] = frames.astype(BF)
            rows[g * EXTRA : (g + 1) * EXTRA, lanes] = extra
    attended_extra[...] = rows[: GROUPS * EXTRA].astype(BF)
    branch_extra = dot(attended_extra[...], out_w[...])
    rows[: GROUPS * EXTRA] = branch_extra
    for g in range(GROUPS):
        memory_rows[g * GROUP : (g + 1) * GROUP] = rows[g * EXTRA : g * EXTRA + GROUP]
    memory_out[...] = memory_rows[...].astype(BF)
    residual = packed[...].astype(F32) + dot(attended[...], out_w[...])
    residual_out[...] = residual
    unit, _ = row_stats(residual)
    middle = (unit * middle_gain[...]).astype(BF)
    ff = up_w.shape[1]
    tile = width
    combined = residual
    for c in range(ff // tile):
        columns = slice(c * tile, (c + 1) * tile)
        part, turn = gelu_parts(dot(middle, up_w[:, columns]))
        part = part.astype(BF)
        hidden[:, columns] = part
        slope[:, columns] = turn.astype(BF)
        combined = combined + dot(part, down_w[columns])
    unit, scale = row_stats(combined)
    rows[...] = unit * output_gain[...]
    for j in range(BLOCK):
        result[j] = rows[j * FRAMES : (j + 1) * FRAMES].astype(BF)
    pack_rows(out_grad, rows, BLOCK)
    grad_combined, gain_part = norm_back(unit, scale, output_gain[...], rows[...])
    grad_combined_out[...] = grad_combined
    grad_ff = grad_combined.astype(BF)

    @pl.when(step == 0)
    def _():
        grad_gain[...] = gain_part
        for c in range(ff // tile):
            down_sum[c * tile : (c + 1) * tile] = dot_outer(hidden[:, c * tile : (c + 1) * tile], grad_ff)

    @pl.when(step > 0)
    def _():
        grad_gain[...] += gain_part
        for c in range(ff // tile):
            down_sum[c * tile : (c + 1) * tile] += dot_outer(hidden[:, c * tile : (c + 1) * tile], grad_ff)

    @pl.when(step == steps - 1)
    def _():
        grad_down[...] = down_sum[...].astype(BF)


def backward_kernel(
    slope, grad_combined, residual, attended, attended_extra, memory_grad, out_w, up_w, down_w, middle_gain,
    grad_residual_out, grad_attended, grad_attended_extra, grad_up, grad_out, grad_gain,
    up_sum, out_sum, rows,
):
    step = pl.program_id(0)
    steps = pl.num_programs(0)

    @pl.when(step == 0)
    def _():
        up_sum[...] = jnp.zeros_like(up_sum)
        out_sum[...] = jnp.zeros_like(out_sum)
        grad_gain[...] = jnp.zeros_like(grad_gain)

    width = residual.shape[1]
    ff = up_w.shape[1]
    tile = width
    unit, scale = row_stats(residual[...])
    middle = (unit * middle_gain[...]).astype(BF)
    grad_combined_rows = grad_combined[...]
    grad_ff = grad_combined_rows.astype(BF)
    grad_middle = jnp.zeros_like(unit)
    for c in range(ff // tile):
        columns = slice(c * tile, (c + 1) * tile)
        lifted = (dot_back(grad_ff, down_w[columns]) * slope[:, columns].astype(F32)).astype(BF)
        up_sum[:, columns] += dot_outer(middle, lifted)
        grad_middle = grad_middle + dot_back(lifted, up_w[:, columns])
    grad_norm, gain_part = norm_back(unit, scale, middle_gain[...], grad_middle)
    grad_gain[...] += gain_part
    grad_residual = grad_combined_rows + grad_norm
    grad_residual_out[...] = grad_residual
    grad_branch = grad_residual.astype(BF)
    memory_rows = memory_grad[...].astype(F32)
    for g in range(GROUPS):
        rows[g * EXTRA : g * EXTRA + GROUP] = memory_rows[g * GROUP : (g + 1) * GROUP]
        rows[g * EXTRA + GROUP : (g + 1) * EXTRA] = jnp.zeros((EXTRA - GROUP, width), F32)
    extra = rows[...].astype(BF)
    out_sum[...] += dot_outer(attended[...], grad_branch) + dot_outer(attended_extra[...], extra)
    grad_attended[...] = dot_back(grad_branch, out_w[...]).astype(BF)
    back_extra = dot_back(extra, out_w[...])
    for g in range(GROUPS):
        part = back_extra[g * EXTRA : (g + 1) * EXTRA]
        grad_attended_extra[2 * g * EXTRA : 2 * (g + 1) * EXTRA] = jnp.concatenate([part, part], axis=0).astype(BF)

    @pl.when(step == steps - 1)
    def _():
        grad_up[...] = up_sum[...].astype(BF)
        grad_out[...] = out_sum[...].astype(BF)


def attention_back_kernel(
    head, query, query_extra, window, soft, grad_attended, grad_attended_extra,
    grad_query, grad_query_extra, pair_sum, pair_memory, halo_back, memory_back,
    rows,
):
    step = pl.program_id(0)
    width = query.shape[1]
    low = low_lanes()
    head_mask = head[...]

    @pl.when(step == 0)
    def _():
        pair_sum[...] = jnp.zeros_like(pair_sum)

    for g in range(GROUPS):
        start = pl.multiple_of((step * GROUPS + g) * GROUP_ROWS, GROUP_ROWS)
        for p in range(PAIRS):
            lanes = slice(p * PAIR, (p + 1) * PAIR)
            value_lanes = slice(width + p * PAIR, width + (p + 1) * PAIR)
            keys = window[g * WINDOW : (g + 1) * WINDOW, lanes]
            values = window[g * WINDOW : (g + 1) * WINDOW, value_lanes]
            stack = query_stack(
                query[g * GROUP_ROWS : (g + 1) * GROUP_ROWS, lanes],
                query_extra[2 * g * EXTRA : 2 * (g + 1) * EXTRA, lanes],
                head_mask,
            )
            grads = query_stack(
                grad_attended[g * GROUP_ROWS : (g + 1) * GROUP_ROWS, lanes],
                grad_attended_extra[2 * g * EXTRA : 2 * (g + 1) * EXTRA, lanes],
                head_mask,
            )
            at = (g * PAIRS + p) * STACK
            soft_low = soft[at : at + STACK]
            soft_wide = soft_low.astype(F32)
            grad_soft = dot_back(grads, values)
            weighted = grad_soft * soft_wide
            grad_scores = (weighted - soft_wide * jnp.sum(weighted, axis=-1, keepdims=True)).astype(BF)
            frames, extra = unstack(dot(grad_scores, keys), low)
            grad_query[g * GROUP_ROWS : (g + 1) * GROUP_ROWS, lanes] = frames.astype(BF)
            rows[g * EXTRA : (g + 1) * EXTRA, lanes] = extra
            grad_keys = dot_outer(grad_scores, stack)
            grad_values = dot_outer(soft_low, grads)
            own = GROUP_ROWS + HALO
            pair_sum[pl.ds(start, own), lanes] += grad_keys[:own]
            pair_sum[pl.ds(start, own), value_lanes] += grad_values[:own]
            pair_memory[g * 2 * MEMS : (g + 1) * 2 * MEMS, lanes] = grad_keys[own:]
            pair_memory[g * 2 * MEMS : (g + 1) * 2 * MEMS, value_lanes] = grad_values[own:]
    grad_query_extra[...] = rows[...].astype(BF)

    @pl.when(step == 0)
    def _():
        halo_back[...] = pair_sum[:HALO].astype(BF)
        memory_back[...] = pair_memory[: 2 * MEMS].astype(BF)


def projection_back_kernel(
    pair_sum, pair_memory, memory_next, halo_next, memory_halo_next,
    grad_query_rows, grad_query_extra, shared, summary, memory, packed, grad_residual,
    query_w, key_w, value_w, gain,
    grad_frames, grad_memory, grad_query, grad_key, grad_value, grad_gain,
    query_sum, key_sum, value_sum, rows,
):
    step = pl.program_id(0)
    steps = pl.num_programs(0)

    @pl.when(step == 0)
    def _():
        query_sum[...] = jnp.zeros_like(query_sum)
        key_sum[...] = jnp.zeros_like(key_sum)
        value_sum[...] = jnp.zeros_like(value_sum)
        grad_gain[...] = jnp.zeros_like(grad_gain)

    last = step == steps - 1
    width = shared.shape[1]
    start = pl.multiple_of(step * ROWS + HALO, 8)
    pair = pair_sum[pl.ds(start, ROWS)]
    late = jnp.where(last, halo_next[...].astype(F32), 0.0)
    pair = jnp.concatenate([pair[: ROWS - HALO], pair[ROWS - HALO :] + late], axis=0).astype(BF)
    memory_late = jnp.where(last, memory_halo_next[...].astype(F32), memory_next[...])
    memory_pair = []
    for g in range(GROUPS):
        this = pair_memory[g * 2 * MEMS + MEMS : (g + 1) * 2 * MEMS]
        if g + 1 < GROUPS:
            after = pair_memory[(g + 1) * 2 * MEMS : (g + 1) * 2 * MEMS + MEMS]
        else:
            after = memory_late[:MEMS]
        memory_pair.append(this + after)
    memory_pair = jnp.concatenate(memory_pair, axis=0).astype(BF)
    grad_keys, grad_values = pair[:, :width], pair[:, width:]
    memory_keys, memory_values = memory_pair[:, :width], memory_pair[:, width:]
    own, extra, own_memory = shared[...], summary[...].astype(BF), memory[...]
    queries, extra_queries = grad_query_rows[...], grad_query_extra[...]
    query_sum[...] += dot_outer(own, queries) + dot_outer(extra, extra_queries)
    key_sum[...] += dot_outer(own, grad_keys) + dot_outer(own_memory, memory_keys)
    value_sum[...] += dot_outer(own, grad_values) + dot_outer(own_memory, memory_values)
    back = dot_back(queries, query_w[...]) * 0.125 + dot_back(grad_keys, key_w[...]) + dot_back(grad_values, value_w[...])
    grad_memory[...] = (dot_back(memory_keys, key_w[...]) + dot_back(memory_values, value_w[...])).astype(BF)
    summary_back = dot_back(extra_queries, query_w[...]) * (0.125 / SEGLEN)
    rows[...] = back
    for j in range(BLOCK):
        spot = j // GROUP * EXTRA + j % GROUP
        rows[j * FRAMES + RIGHT : (j + 1) * FRAMES] += summary_back[spot : spot + 1]
    unit, scale = row_stats(packed[...].astype(F32))
    grad_norm, gain_part = norm_back(unit, scale, gain[...], rows[...])
    grad_gain[...] += gain_part
    rows[...] = grad_residual[...] + grad_norm
    for j in range(BLOCK):
        grad_frames[j] = rows[j * FRAMES : (j + 1) * FRAMES]

    @pl.when(last)
    def _():
        grad_query[...] = (query_sum[...] * 0.125).astype(BF)
        grad_key[...] = key_sum[...].astype(BF)
        grad_value[...] = value_sum[...].astype(BF)


def whole(shape):
    return pl.BlockSpec(shape, lambda i: (0,) * len(shape))


def rows_of(*shape):
    return pl.BlockSpec(shape, lambda i: (i,) + (0,) * (len(shape) - 1))


def params():
    return pltpu.CompilerParams(vmem_limit_bytes=VMEM_LIMIT)


def shape_of(dtype, *shape):
    return jax.ShapeDtypeStruct(shape, dtype)


def segment_position(counts_row, segment):
    order = jnp.arange(counts_row.shape[0], dtype=jnp.int32)
    starts = jnp.sum(jnp.where(order[None, :] < order[:, None], counts_row[None, :], 0), axis=1)
    first = jnp.max(jnp.where(starts[None, :] <= segment[:, None], starts[None, :], 0), axis=1)
    return segment - first


def shift(values, axis, by):
    size = lax.axis_size(axis)
    return lax.ppermute(values, axis, [(i, (i + by) % size) for i in range(size)])


def swap(values, axis, bit):
    size = lax.axis_size(axis)
    return lax.ppermute(values, axis, [(i, i ^ bit) for i in range(size)])


def axis_bits(axis):
    size = lax.axis_size(axis)
    return [1 << i for i in range(size.bit_length() - 1)]


def sum_everywhere(values):
    dtype = values.dtype
    steps = [("grp", b) for b in axis_bits("grp")] + [("seg", b) for b in axis_bits("seg")]
    sides = []
    for axis, bit in steps:
        side = (lax.axis_index(axis) // bit) % 2
        half = values.shape[0] // 2
        keep = lax.dynamic_slice_in_dim(values, side * half, half, 0)
        send = lax.dynamic_slice_in_dim(values, (1 - side) * half, half, 0)
        values = (keep.astype(F32) + swap(send, axis, bit).astype(F32)).astype(dtype)
        sides.append(side)
    for (axis, bit), side in zip(reversed(steps), reversed(sides)):
        other = swap(values, axis, bit)
        values = jnp.where(
            side == 0, jnp.concatenate([values, other], axis=0), jnp.concatenate([other, values], axis=0)
        )
    return values


def sum_small(values):
    for axis in ("grp", "seg"):
        for bit in axis_bits(axis):
            values = values + swap(values, axis, bit)
    return values


def per_device(
    frames_in, memory, counts, query_weight, key_weight, value_weight, out_weight, up_weight, down_weight,
    input_gain, middle_gain, output_gain, out_grad, memory_grad,
):
    slots, _, width = frames_in.shape
    ff = up_weight.shape[1]
    steps = slots // BLOCK
    total = slots * FRAMES
    groups = slots // GROUP
    grid = (steps,)
    need, segment_of, head = stack_tables()
    need, segment_of, head = jnp.asarray(need), jnp.asarray(segment_of), jnp.asarray(head, BF)
    input_gain, middle_gain, output_gain = (g.reshape(1, width) for g in (input_gain, middle_gain, output_gain))
    segment = lax.axis_index("seg") * slots + jnp.arange(slots, dtype=jnp.int32)
    position = segment_position(counts[0], segment)
    halo = shift(frames_in[slots - 2 :], "seg", 1)
    memory_halo = shift(memory[slots - 8 :], "seg", 1)

    packed, shared, summary, query, query_extra, window = pl.pallas_call(
        project_kernel,
        grid=grid,
        in_specs=[
            rows_of(BLOCK, FRAMES, width),
            pl.BlockSpec((2, FRAMES, width), lambda i: (jnp.maximum(i * (BLOCK // 2) - 1, 0), 0, 0)),
            whole((2, FRAMES, width)),
            whole((slots, width)),
            whole((8, width)),
            whole((1, width)),
            whole((width, width)),
            whole((width, width)),
            whole((width, width)),
        ],
        out_specs=[
            rows_of(ROWS, width),
            rows_of(ROWS, width),
            rows_of(GROUPS * EXTRA, width),
            rows_of(ROWS, width),
            rows_of(2 * GROUPS * EXTRA, width),
            rows_of(GROUPS * WINDOW, 2 * width),
        ],
        out_shape=[
            shape_of(BF, total, width),
            shape_of(BF, total, width),
            shape_of(F32, groups * EXTRA, width),
            shape_of(BF, total, width),
            shape_of(BF, 2 * groups * EXTRA, width),
            shape_of(BF, groups * WINDOW, 2 * width),
        ],
        scratch_shapes=[pltpu.VMEM((ROWS + HALO, width), F32), pltpu.VMEM((slots + 8, width), F32)],
        compiler_params=params(),
        name="project",
    )(frames_in, frames_in, halo, memory, memory_halo, input_gain, query_weight, key_weight, value_weight)

    (
        attended, attended_extra, soft, residual, slope, grad_combined, result, memory_out, grad_down, output_part,
    ) = pl.pallas_call(
        forward_kernel,
        grid=grid,
        in_specs=[
            pl.BlockSpec(memory_space=pltpu.SMEM),
            whole((STACK, WINDOW)),
            whole((STACK, WINDOW)),
            whole((STACK, PAIR)),
            rows_of(ROWS, width),
            rows_of(2 * GROUPS * EXTRA, width),
            rows_of(GROUPS * WINDOW, 2 * width),
            rows_of(ROWS, width),
            rows_of(BLOCK, FRAMES, width),
            whole((width, width)),
            whole((width, ff)),
            whole((ff, width)),
            whole((1, width)),
            whole((1, width)),
        ],
        out_specs=[
            rows_of(ROWS, width),
            rows_of(GROUPS * EXTRA, width),
            rows_of(GROUPS * PAIRS * STACK, WINDOW),
            rows_of(ROWS, width),
            rows_of(ROWS, ff),
            rows_of(ROWS, width),
            rows_of(BLOCK, FRAMES, width),
            rows_of(BLOCK, width),
            whole((ff, width)),
            whole((1, width)),
        ],
        out_shape=[
            shape_of(BF, total, width),
            shape_of(BF, groups * EXTRA, width),
            shape_of(BF, groups * PAIRS * STACK, WINDOW),
            shape_of(F32, total, width),
            shape_of(BF, total, ff),
            shape_of(F32, total, width),
            shape_of(BF, slots, FRAMES, width),
            shape_of(BF, slots, width),
            shape_of(BF, ff, width),
            shape_of(F32, 1, width),
        ],
        scratch_shapes=[
            pltpu.VMEM((ROWS, width), F32),
            pltpu.VMEM((ff, width), F32),
            pltpu.VMEM((ROWS, ff), BF),
            pltpu.VMEM((BLOCK, width), F32),
        ],
        compiler_params=params(),
        name="forward",
    )(
        position, need, segment_of, head, query, query_extra, window, packed, out_grad,
        out_weight, up_weight, down_weight, middle_gain, output_gain,
    )

    grad_residual, grad_attended, grad_attended_extra, grad_up, grad_out, middle_part = pl.pallas_call(
        backward_kernel,
        grid=grid,
        in_specs=[
            rows_of(ROWS, ff),
            rows_of(ROWS, width),
            rows_of(ROWS, width),
            rows_of(ROWS, width),
            rows_of(GROUPS * EXTRA, width),
            rows_of(BLOCK, width),
            whole((width, width)),
            whole((width, ff)),
            whole((ff, width)),
            whole((1, width)),
        ],
        out_specs=[
            rows_of(ROWS, width),
            rows_of(ROWS, width),
            rows_of(2 * GROUPS * EXTRA, width),
            whole((width, ff)),
            whole((width, width)),
            whole((1, width)),
        ],
        out_shape=[
            shape_of(F32, total, width),
            shape_of(BF, total, width),
            shape_of(BF, 2 * groups * EXTRA, width),
            shape_of(BF, width, ff),
            shape_of(BF, width, width),
            shape_of(F32, 1, width),
        ],
        scratch_shapes=[
            pltpu.VMEM((width, ff), F32),
            pltpu.VMEM((width, width), F32),
            pltpu.VMEM((GROUPS * EXTRA, width), F32),
        ],
        compiler_params=params(),
        name="backward",
    )(slope, grad_combined, residual, attended, attended_extra, memory_grad, out_weight, up_weight, down_weight, middle_gain)

    grad_query_rows, grad_query_extra, pair_sum, pair_memory, halo_back, memory_back = pl.pallas_call(
        attention_back_kernel,
        grid=grid,
        in_specs=[
            whole((STACK, PAIR)),
            rows_of(ROWS, width),
            rows_of(2 * GROUPS * EXTRA, width),
            rows_of(GROUPS * WINDOW, 2 * width),
            rows_of(GROUPS * PAIRS * STACK, WINDOW),
            rows_of(ROWS, width),
            rows_of(2 * GROUPS * EXTRA, width),
        ],
        out_specs=[
            rows_of(ROWS, width),
            rows_of(GROUPS * EXTRA, width),
            whole((total + HALO, 2 * width)),
            rows_of(GROUPS * 2 * MEMS, 2 * width),
            whole((HALO, 2 * width)),
            whole((2 * MEMS, 2 * width)),
        ],
        out_shape=[
            shape_of(BF, total, width),
            shape_of(BF, groups * EXTRA, width),
            shape_of(F32, total + HALO, 2 * width),
            shape_of(F32, groups * 2 * MEMS, 2 * width),
            shape_of(BF, HALO, 2 * width),
            shape_of(BF, 2 * MEMS, 2 * width),
        ],
        scratch_shapes=[pltpu.VMEM((GROUPS * EXTRA, width), F32)],
        compiler_params=params(),
        name="attention_back",
    )(head, query, query_extra, window, soft, grad_attended, grad_attended_extra)

    halo_next = shift(halo_back, "seg", -1)
    memory_halo_next = shift(memory_back, "seg", -1)

    grad_frames, grad_memory, grad_query, grad_key, grad_value, input_part = pl.pallas_call(
        projection_back_kernel,
        grid=grid,
        in_specs=[
            whole((total + HALO, 2 * width)),
            rows_of(GROUPS * 2 * MEMS, 2 * width),
            pl.BlockSpec((2 * MEMS, 2 * width), lambda i: (jnp.minimum((i + 1) * GROUPS, groups - 1), 0)),
            whole((HALO, 2 * width)),
            whole((2 * MEMS, 2 * width)),
            rows_of(ROWS, width),
            rows_of(GROUPS * EXTRA, width),
            rows_of(ROWS, width),
            rows_of(GROUPS * EXTRA, width),
            rows_of(BLOCK, width),
            rows_of(ROWS, width),
            rows_of(ROWS, width),
            whole((width, width)),
            whole((width, width)),
            whole((width, width)),
            whole((1, width)),
        ],
        out_specs=[
            rows_of(BLOCK, FRAMES, width),
            rows_of(BLOCK, width),
            whole((width, width)),
            whole((width, width)),
            whole((width, width)),
            whole((1, width)),
        ],
        out_shape=[
            shape_of(F32, slots, FRAMES, width),
            shape_of(BF, slots, width),
            shape_of(BF, width, width),
            shape_of(BF, width, width),
            shape_of(BF, width, width),
            shape_of(F32, 1, width),
        ],
        scratch_shapes=[
            pltpu.VMEM((width, width), F32),
            pltpu.VMEM((width, width), F32),
            pltpu.VMEM((width, width), F32),
            pltpu.VMEM((ROWS, width), F32),
        ],
        compiler_params=params(),
        name="projection_back",
    )(
        pair_sum, pair_memory, pair_memory, halo_next, memory_halo_next,
        grad_query_rows, grad_query_extra, shared, summary, memory, packed, grad_residual,
        query_weight, key_weight, value_weight, input_gain,
    )

    grad_down = sum_everywhere(grad_down).astype(F32)
    grad_up = sum_everywhere(grad_up).astype(F32)
    squares = sum_everywhere(jnp.concatenate([grad_out, grad_query, grad_key, grad_value], axis=0)).astype(F32)
    grad_out, grad_query, grad_key, grad_value = jnp.split(squares, 4)
    gains = sum_small(jnp.concatenate([input_part, middle_part, output_part], axis=0))
    return (
        result, memory_out, grad_frames, grad_memory,
        grad_query, grad_key, grad_value, grad_out, grad_up, grad_down,
        gains[0], gains[1], gains[2],
    )


def solution(mesh):
    rows = P(("grp", "seg"), None, None)
    singles = P(("grp", "seg"), None)
    return jax.shard_map(
        per_device,
        mesh=mesh,
        in_specs=(rows, singles, P("grp", None)) + (P(),) * 9 + (rows, singles),
        out_specs=(rows, singles, rows, singles) + (P(),) * 9,
        check_vma=False,
    )
```

```python
import jax
import jax.numpy as jnp
import numpy as np
from jax import lax
from jax.experimental import pallas as pl
from jax.experimental.pallas import tpu as pltpu
from jax.sharding import PartitionSpec as P

HEADS = 8
HDIM = 64
SEGLEN = 16
RIGHT = 4
LEFT = 30
MEMS = 4
FRAMES = RIGHT + SEGLEN

GROUP = 4
TILE = 128
PART = 8
PART_FRAMES = FRAMES * PART
PART_ROWS = PART_FRAMES + 2 * PART
PART_TILES = PART // GROUP * TILE
CARRY = 48
CARRY_FRAMES = 2 * FRAMES
BLOCK = 16
PARTS = BLOCK // PART
ROWS = BLOCK * FRAMES
FULL = PARTS * PART_ROWS
TILES = PARTS * PART_TILES
PAIRS = HEADS // 2
PAIR = 2 * HDIM

EPSILON = 1e-05
MASKED_SCORE = -1e30
FAR = 1 << 20

BF = jnp.bfloat16
F32 = jnp.float32
VMEM_LIMIT = 60 * 1024 * 1024


def dot(a, b):
    return lax.dot_general(a, b, (((1,), (0,)), ((), ())), preferred_element_type=F32)


def dot_back(a, b):
    return lax.dot_general(a, b, (((1,), (1,)), ((), ())), preferred_element_type=F32)


def dot_outer(a, b):
    return lax.dot_general(a, b, (((0,), (0,)), ((), ())), preferred_element_type=F32)


def tables():
    pick_query = np.zeros((PART_TILES, PART_ROWS), np.float32)
    pick_key = np.zeros((PART_TILES, PART_ROWS + CARRY), np.float32)
    pick_carry = np.zeros((CARRY, PART_ROWS), np.float32)
    for group in range(PART // GROUP):
        for row in range(GROUP * FRAMES):
            segment = group * GROUP + row // FRAMES
            pick_query[group * TILE + row, row % FRAMES * PART + segment] = 1
        for row in range(GROUP):
            pick_query[group * TILE + GROUP * FRAMES + row, PART_FRAMES + group * GROUP + row] = 1
        for row in range((GROUP + 2) * FRAMES):
            segment, frame = group * GROUP - 2 + row // FRAMES, row % FRAMES
            column = frame * PART + segment if segment >= 0 else PART_ROWS + frame * 2 + segment + 2
            pick_key[group * TILE + row, column] = 1
        for row in range(GROUP + MEMS):
            segment = group * GROUP - MEMS + row
            column = PART_FRAMES + segment if segment >= 0 else PART_ROWS + CARRY_FRAMES + segment + MEMS
            pick_key[group * TILE + (GROUP + 2) * FRAMES + row, column] = 1
    for frame in range(FRAMES):
        for back in range(2):
            pick_carry[frame * 2 + back, frame * PART + PART - 2 + back] = 1
    for back in range(MEMS):
        pick_carry[CARRY_FRAMES + back, PART_FRAMES + PART - MEMS + back] = 1
    row = np.arange(TILE)
    is_summary = (row >= GROUP * FRAMES) & (row < GROUP * FRAMES + GROUP)
    segment = np.where(is_summary, row - GROUP * FRAMES, np.where(row < GROUP * FRAMES, row // FRAMES, 0))
    is_memory = row >= (GROUP + 2) * FRAMES
    key_segment = np.where(is_memory, row - (GROUP + 2) * FRAMES - MEMS, row // FRAMES - 2)
    within = row % FRAMES
    is_right = ~is_memory & (within < RIGHT)
    behind = segment[None, :] - key_segment[:, None]
    late = (within >= RIGHT + 2 * SEGLEN - LEFT)[:, None]
    frame_ok = (behind == 0) | (~is_right[:, None] & ((behind == 1) | ((behind == 2) & late)))
    memory_ok = (behind >= 1) & (behind <= MEMS) & ~is_summary[None, :]
    need = np.where(np.where(is_memory[:, None], memory_ok, frame_ok), behind, FAR).astype(np.int32)
    segment_of = np.ascontiguousarray(np.broadcast_to(segment[None, :], (TILE, TILE))).astype(np.int32)
    return pick_query, pick_key, pick_carry, need, segment_of


def row_stats(values):
    centered = values - jnp.mean(values, axis=-1, keepdims=True)
    spread = jnp.mean(centered * centered, axis=-1, keepdims=True)
    scale = lax.rsqrt(spread + EPSILON)
    return centered * scale, scale


def norm_back(unit, scale, gain, gradient):
    gained = gradient * gain
    along = jnp.mean(gained * unit, axis=-1, keepdims=True)
    grad = scale * (gained - jnp.mean(gained, axis=-1, keepdims=True) - unit * along)
    return grad, jnp.sum(gradient * unit, axis=0, keepdims=True)


def by_part(slabs):
    frames, _, width = slabs.shape
    return [slabs[:, p * PART : (p + 1) * PART].reshape(frames * PART, width) for p in range(PARTS)]


def by_frame(parts):
    return jnp.concatenate([part.reshape(FRAMES, PART, part.shape[1]) for part in parts], axis=1)


def project_kernel(
    frames, memory, halo, gain, query_w, key_w, value_w, pick_query, pick_key, pick_carry,
    query_rows, key_rows, query, window,
    carry_rows, carry_pair,
):
    step = pl.program_id(0)
    width = query_w.shape[0]

    @pl.when(step == 0)
    def _():
        raw = halo[...].astype(F32)
        unit, _ = row_stats(raw)
        is_frame = lax.broadcasted_iota(jnp.int32, raw.shape, 0) < CARRY_FRAMES
        carried = jnp.where(is_frame, unit * gain[...], raw).astype(BF)
        carry_rows[...] = carried
        carry_pair[:, :width] = dot(carried, key_w[...]).astype(BF)
        carry_pair[:, width:] = dot(carried, value_w[...]).astype(BF)

    memories = memory[...].astype(F32)
    for p, part in enumerate(by_part(frames[...].astype(F32))):
        unit, _ = row_stats(part)
        normed = unit * gain[...]
        mean = normed[RIGHT * PART : (RIGHT + 1) * PART]
        for f in range(RIGHT + 1, FRAMES):
            mean = mean + normed[f * PART : (f + 1) * PART]
        mean = mean * (1.0 / SEGLEN)
        blank = jnp.zeros_like(mean)
        asks = jnp.concatenate([normed, mean, blank], axis=0).astype(BF)
        keys = jnp.concatenate([normed, memories[p * PART : (p + 1) * PART], blank], axis=0).astype(BF)
        query_rows[p * PART_ROWS : (p + 1) * PART_ROWS] = asks
        at = p * (PART_ROWS + CARRY)
        key_rows[at : at + PART_ROWS] = keys
        key_rows[at + PART_ROWS : at + PART_ROWS + CARRY] = carry_rows[...]
        asked = (dot(asks, query_w[...]) * 0.125).astype(BF)
        query[p * PART_TILES : (p + 1) * PART_TILES] = dot(pick_query[...], asked).astype(BF)
        pair = jnp.concatenate([dot(keys, key_w[...]), dot(keys, value_w[...])], axis=1).astype(BF)
        both = jnp.concatenate([pair, carry_pair[...]], axis=0)
        window[p * PART_TILES : (p + 1) * PART_TILES] = dot(pick_key[...], both).astype(BF)
        carry_rows[...] = dot(pick_carry[...], keys).astype(BF)
        carry_pair[...] = dot(pick_carry[...], pair).astype(BF)


def two_heads(rows):
    low = lax.broadcasted_iota(jnp.int32, (1, PAIR), 1) < HDIM
    wide = rows.astype(F32)
    return jnp.concatenate([jnp.where(low, wide, 0.0), jnp.where(low, 0.0, wide)], axis=0).astype(BF)


def of_two_heads(columns):
    return jnp.concatenate([columns[:HDIM, :TILE], columns[HDIM:, TILE:]], axis=0).astype(BF)


def gelu_parts(lifted):
    bell = jnp.exp(lifted * lifted * -0.5) * 0.3989422804014327
    share = 0.5 + 0.5 * lax.erf(lifted * 0.7071067811865476)
    return lifted * share, share + lifted * bell


def forward_kernel(
    position, need, segment_of, unpick_query, query, window, frames, out_grad,
    out_w, up_w, down_w, middle_gain, output_gain,
    attended, soft, residual_out, slope, grad_combined_out, result, memory_out, grad_down, grad_gain,
    turned, hidden, grad_ff_rows,
):
    step = pl.program_id(0)
    steps = pl.num_programs(0)
    width = out_w.shape[0]
    ff = up_w.shape[1]
    for p in range(PARTS):
        for g in range(PART // GROUP):
            tile = p * (PART // GROUP) + g
            first = step * BLOCK + tile * GROUP
            column = segment_of[...]
            at = jnp.where(
                column < 2,
                jnp.where(column == 0, position[first], position[first + 1]),
                jnp.where(column == 2, position[first + 2], position[first + 3]),
            )
            bias = jnp.where(at >= need[...], 0.0, MASKED_SCORE)
            bias = jnp.concatenate([bias, bias], axis=1)
            rows = slice(tile * TILE, (tile + 1) * TILE)
            for h in range(PAIRS):
                lanes = slice(h * PAIR, (h + 1) * PAIR)
                keys = window[rows, lanes]
                values = window[rows, width + h * PAIR : width + (h + 1) * PAIR]
                scores = dot_back(keys, two_heads(query[rows, lanes])) + bias
                powers = jnp.exp(scores - jnp.max(scores, axis=0, keepdims=True))
                soft_low = (powers * (1.0 / jnp.sum(powers, axis=0, keepdims=True))).astype(BF)
                spot = (tile * PAIRS + h) * TILE
                soft[spot : spot + TILE] = soft_low
                turned[lanes, g * TILE : (g + 1) * TILE] = of_two_heads(dot_outer(values, soft_low))
        attended[p * PART_ROWS : (p + 1) * PART_ROWS] = dot_back(unpick_query[...], turned[...]).astype(BF)
    branch = dot(attended[...], out_w[...])
    own = frames[...].astype(F32)
    residual, memory_rows = [], []
    for p, part in enumerate(by_part(own)):
        at = p * PART_ROWS
        residual.append(part + branch[at : at + PART_FRAMES])
        memory_rows.append(branch[at + PART_FRAMES : at + PART_FRAMES + PART])
    memory_out[...] = jnp.concatenate(memory_rows, axis=0).astype(BF)
    residual = jnp.concatenate(residual, axis=0)
    residual_out[...] = residual
    unit, _ = row_stats(residual)
    middle = (unit * middle_gain[...]).astype(BF)
    combined = residual
    span = pl.ds(pl.multiple_of(step * ROWS, ROWS), ROWS)
    for c in range(ff // width):
        columns = slice(c * width, (c + 1) * width)
        part, turn = gelu_parts(dot(middle, up_w[:, columns]))
        part = part.astype(BF)
        hidden[span, columns] = part
        slope[:, columns] = turn.astype(BF)
        combined = combined + dot(part, down_w[columns])
    unit, scale = row_stats(combined)
    final = unit * output_gain[...]
    result[...] = by_frame([final[p * PART_FRAMES : (p + 1) * PART_FRAMES] for p in range(PARTS)]).astype(BF)
    pulled = jnp.concatenate(by_part(out_grad[...].astype(F32)), axis=0)
    grad_combined, gain_part = norm_back(unit, scale, output_gain[...], pulled)
    grad_combined_out[...] = grad_combined
    grad_ff_rows[span] = grad_combined.astype(BF)

    @pl.when(step == 0)
    def _():
        grad_gain[...] = gain_part

    @pl.when(step > 0)
    def _():
        grad_gain[...] += gain_part

    @pl.when(step == steps - 1)
    def _():
        for c in range(ff // width):
            columns = slice(c * width, (c + 1) * width)
            grad_down[columns] = dot_outer(hidden[:, columns], grad_ff_rows[...]).astype(BF)


def backward_kernel(
    slope, grad_combined, residual, attended, memory_grad, out_w, up_w, down_w, middle_gain,
    grad_residual_out, grad_attended, grad_up_out, grad_gain,
    lifted, middle_rows, out_sum,
):
    step = pl.program_id(0)
    steps = pl.num_programs(0)
    width = out_w.shape[0]
    ff = up_w.shape[1]
    span = pl.ds(pl.multiple_of(step * ROWS, ROWS), ROWS)
    unit, scale = row_stats(residual[...])
    middle_rows[span] = (unit * middle_gain[...]).astype(BF)
    grad_combined_rows = grad_combined[...]
    grad_ff = grad_combined_rows.astype(BF)
    grad_middle = jnp.zeros_like(unit)
    for c in range(ff // width):
        columns = slice(c * width, (c + 1) * width)
        part = (dot_back(grad_ff, down_w[columns]) * slope[:, columns].astype(F32)).astype(BF)
        lifted[span, columns] = part
        grad_middle = grad_middle + dot_back(part, up_w[:, columns])
    grad_norm, gain_part = norm_back(unit, scale, middle_gain[...], grad_middle)
    grad_residual = grad_combined_rows + grad_norm
    grad_residual_out[...] = grad_residual
    memory_rows = memory_grad[...].astype(F32)
    blank = jnp.zeros((PART, width), F32)
    grad_branch = []
    for p in range(PARTS):
        grad_branch += [grad_residual[p * PART_FRAMES : (p + 1) * PART_FRAMES], memory_rows[p * PART : (p + 1) * PART], blank]
    grad_branch = jnp.concatenate(grad_branch, axis=0).astype(BF)
    grad_attended[...] = dot_back(grad_branch, out_w[...]).astype(BF)
    out_part = dot_outer(attended[...], grad_branch)

    @pl.when(step == 0)
    def _():
        grad_gain[...] = gain_part
        out_sum[...] = out_part

    @pl.when(step > 0)
    def _():
        grad_gain[...] += gain_part
        out_sum[...] += out_part

    @pl.when(step == steps - 1)
    def _():
        grad_up_out[:, ff:] = out_sum[...].astype(BF)
        for c in range(ff // width):
            columns = slice(c * width, (c + 1) * width)
            grad_up_out[:, columns] = dot_outer(middle_rows[...], lifted[:, columns]).astype(BF)


def attention_back_kernel(
    pick_query, unpick_query, unpick_key, query_rows, key_rows, query, window, soft, grad_attended,
    grad_query_rows, grad_pair, grad_carry, grad_projections,
    turned, grad_window, query_sum, pair_sum,
):
    step = pl.program_id(0)
    steps = pl.num_programs(0)
    width = query.shape[1]

    @pl.when(step == 0)
    def _():
        query_sum[...] = jnp.zeros_like(query_sum)
        pair_sum[...] = jnp.zeros_like(pair_sum)

    for p in range(PARTS):
        pulled = dot(pick_query[...], grad_attended[p * PART_ROWS : (p + 1) * PART_ROWS]).astype(BF)
        for g in range(PART // GROUP):
            tile = p * (PART // GROUP) + g
            rows = slice(tile * TILE, (tile + 1) * TILE)
            spread = slice(g * TILE, (g + 1) * TILE)
            for h in range(PAIRS):
                lanes = slice(h * PAIR, (h + 1) * PAIR)
                value_lanes = slice(width + h * PAIR, width + (h + 1) * PAIR)
                keys = window[rows, lanes]
                values = window[rows, value_lanes]
                asks = two_heads(query[rows, lanes])
                grads = two_heads(pulled[spread, lanes])
                spot = (tile * PAIRS + h) * TILE
                soft_low = soft[spot : spot + TILE]
                soft_wide = soft_low.astype(F32)
                weighted = dot_back(values, grads) * soft_wide
                grad_scores = (weighted - soft_wide * jnp.sum(weighted, axis=0, keepdims=True)).astype(BF)
                grad_window[spread, lanes] = dot(grad_scores, asks).astype(BF)
                grad_window[spread, value_lanes] = dot(soft_low, grads).astype(BF)
                turned[lanes, spread] = of_two_heads(dot_outer(keys, grad_scores))
        part = slice(p * PART_ROWS, (p + 1) * PART_ROWS)
        grad_asks = dot_back(unpick_query[...], turned[...]).astype(BF)
        grad_query_rows[part] = grad_asks
        both = dot(unpick_key[...], grad_window[...]).astype(BF)
        grad_pair[part] = both[:PART_ROWS]
        grad_carry[p * CARRY : (p + 1) * CARRY] = both[PART_ROWS:]
        query_sum[...] += dot_outer(query_rows[part], grad_asks)
        pair_sum[...] += dot_outer(key_rows[p * (PART_ROWS + CARRY) : (p + 1) * (PART_ROWS + CARRY)], both)

    @pl.when(step == steps - 1)
    def _():
        grad_projections[:, :width] = (query_sum[...] * 0.125).astype(BF)
        grad_projections[:, width:] = pair_sum[...].astype(BF)


def projection_back_kernel(
    unpick_carry, grad_pair, grad_carry, carry_next, grad_query_rows, frames, grad_residual, query_w, key_w, value_w, gain,
    grad_frames, grad_memory, grad_gain,
):
    step = pl.program_id(0)
    steps = pl.num_programs(0)
    width = query_w.shape[0]
    pairs = []
    for p in range(PARTS):
        after = step * PARTS + p + 1
        inside = jnp.minimum(after, steps * PARTS - 1)
        late = grad_carry[pl.ds(pl.multiple_of(inside * CARRY, CARRY), CARRY)]
        if p == PARTS - 1:
            late = jnp.where(step == steps - 1, carry_next[...].astype(F32), late.astype(F32)).astype(BF)
        pairs.append(grad_pair[p * PART_ROWS : (p + 1) * PART_ROWS].astype(F32) + dot(unpick_carry[...], late))
    pair = jnp.concatenate(pairs, axis=0).astype(BF)
    query_back = dot_back(grad_query_rows[...], query_w[...]) * 0.125
    key_back = dot_back(pair[:, :width], key_w[...]) + dot_back(pair[:, width:], value_w[...])
    memory_rows, results = [], []
    gain_part = jnp.zeros((1, width), F32)
    for p, part in enumerate(by_part(frames[...].astype(F32))):
        at = p * PART_ROWS
        end = at + PART_FRAMES
        memory_rows.append(key_back[end : end + PART])
        own = query_back[at:end] + key_back[at:end]
        share = query_back[end : end + PART] * (1.0 / SEGLEN)
        share = jnp.concatenate([jnp.zeros((RIGHT * PART, width), F32)] + [share] * SEGLEN, axis=0)
        unit, scale = row_stats(part)
        grad_norm, more = norm_back(unit, scale, gain[...], own + share)
        gain_part = gain_part + more
        results.append(grad_residual[p * PART_FRAMES : (p + 1) * PART_FRAMES] + grad_norm)
    grad_frames[...] = by_frame(results)
    grad_memory[...] = jnp.concatenate(memory_rows, axis=0).astype(BF)

    @pl.when(step == 0)
    def _():
        grad_gain[...] = gain_part

    @pl.when(step > 0)
    def _():
        grad_gain[...] += gain_part


def cost(us):
    return pl.CostEstimate(flops=int(us * 1e9), bytes_accessed=int(us * 1e5), transcendentals=0)


def segment_position(counts_row, segment):
    order = jnp.arange(counts_row.shape[0], dtype=jnp.int32)
    starts = jnp.sum(jnp.where(order[None, :] < order[:, None], counts_row[None, :], 0), axis=1)
    first = jnp.max(jnp.where(starts[None, :] <= segment[:, None], starts[None, :], 0), axis=1)
    return segment - first


def shift(values, axis, by):
    size = lax.axis_size(axis)
    return lax.ppermute(values, axis, [(i, (i + by) % size) for i in range(size)])


def axis_bits(axis):
    return [1 << i for i in range(lax.axis_size(axis).bit_length() - 1)]


def chain(turn):
    bits = axis_bits("seg")
    few = min(3, len(bits))

    def turned(by):
        by = by % max(1, few)
        return bits[by:few] + bits[:by] + bits[few:]

    return ["grp"] + list(zip(turned(turn), turned(turn + 1)))


def side(stage):
    if stage == "grp":
        return lax.axis_index("grp")
    place = lax.axis_index("seg")
    return jnp.where(lax.axis_index("grp") == 0, place // stage[0] % 2, place // stage[1] % 2)


def swap(values, stage):
    if stage == "grp":
        return lax.ppermute(values, "grp", [(0, 1), (1, 0)])
    size = lax.axis_size("seg")
    pairs = [(core * size + i, core * size + (i ^ stage[core])) for core in range(2) for i in range(size)]
    return lax.ppermute(values, ("grp", "seg"), pairs)


def split_sum(total):
    high = total.astype(BF)
    return high, (total - high.astype(F32)).astype(BF)


class Sum:
    def __init__(self, values, turn):
        self.values = values
        self.turn = turn
        self.steps = chain(turn)
        self.done = 0
        self.row = None

    def start(self, tie=None):
        count = len(self.steps)
        if self.done < count:
            stage = self.steps[self.done]
            rows = self.values.shape[0] // 2
            own = side(stage)
            self.values, send = (
                lax.dynamic_slice_in_dim(self.values, half * rows, rows, 0) for half in (own, 1 - own)
            )
        else:
            stage = self.steps[2 * count - 1 - self.done]
            send = self.values
            if self.row is not None:
                blank = jnp.zeros((6, self.row.shape[1]), BF)
                send = jnp.concatenate([send, *split_sum(self.row), blank], axis=0)
        if tie is not None:
            send, _ = lax.optimization_barrier((send, tie))
        self.arriving = swap(send, stage)
        return send

    def land(self, *ties):
        count = len(self.steps)
        other = lax.optimization_barrier((self.arriving,) + ties)[0] if ties else self.arriving
        if self.done < count:
            self.values = (self.values.astype(F32) + other.astype(F32)).astype(self.values.dtype)
        else:
            rows = self.values.shape[0]
            if self.row is not None:
                high, low = split_sum(self.row)
                theirs = other[rows : rows + 1].astype(F32) + other[rows + 1 : rows + 2].astype(F32)
                self.row = high.astype(F32) + low.astype(F32) + theirs
                other = other[:rows]
            if self.done < 2 * count - 1:
                self.values = jnp.concatenate([self.values, other], axis=0)
            else:
                self.other = other
        self.done += 1

    def complete(self):
        return self.done == 2 * len(self.steps)


def shares(turn):
    place = lax.axis_index("seg")
    found = []
    for core in range(2):
        share = 0
        for stage in chain(turn)[1:]:
            share = share * 2 + place // stage[core] % 2
        found.append(share)
    core = lax.axis_index("grp")
    own = jnp.where(core == 0, found[0], found[1])
    other = jnp.where(core == 0, found[1], found[0])
    return jnp.stack([core, own, other])


def finish(total, widths):
    own, other = total.values, total.other
    half = own.shape[0]
    count = lax.axis_size("seg")
    rows = half // count
    place = shares(total.turn)
    cuts = np.cumsum(widths)[:-1].tolist()
    if rows % 16:
        index = jnp.arange(count, dtype=jnp.int32)
        mine, theirs = (
            jnp.take(part.reshape(count, rows, -1), index ^ place[i], axis=0).reshape(half, -1)
            for part, i in ((own, 1), (other, 2))
        )
        whole = jnp.where(place[0] == 0, jnp.concatenate([mine, theirs]), jnp.concatenate([theirs, mine]))
        return jnp.split(whole.astype(F32), cuts, axis=1)
    halves = 2

    def kernel(place_ref, own_ref, other_ref, *outs):
        step = pl.program_id(0)
        mine = (step // halves) == place_ref[0]

        def fill(source, share):
            for j in range(count // halves):
                piece = (step % halves * (count // halves) + j) ^ share
                block = source[pl.ds(pl.multiple_of(piece * rows, rows), rows)].astype(F32)
                at = 0
                for out in outs:
                    out[j * rows : (j + 1) * rows] = block[:, at : at + out.shape[1]]
                    at += out.shape[1]

        @pl.when(mine)
        def _():
            fill(own_ref, place_ref[1])

        @pl.when(jnp.logical_not(mine))
        def _():
            fill(other_ref, place_ref[2])

    return pl.pallas_call(
        kernel,
        grid=(2 * halves,),
        in_specs=[pl.BlockSpec(memory_space=pltpu.SMEM)] + [pl.BlockSpec(own.shape, lambda i: (0, 0))] * 2,
        out_specs=[pl.BlockSpec((half // halves, w), lambda i: (i, 0)) for w in widths],
        out_shape=[jax.ShapeDtypeStruct((2 * half, w), F32) for w in widths],
        compiler_params=pltpu.CompilerParams(vmem_limit_bytes=VMEM_LIMIT),
        cost_estimate=cost(3),
        name="finish",
    )(place, own, other)


def call(kernel, steps, operands, outs, scratch, us):
    def spec(shape, block):
        if isinstance(block, pl.BlockSpec):
            return block
        if block is None:
            return pl.BlockSpec(shape, lambda i: (0,) * len(shape))
        if len(block) == 3:
            return pl.BlockSpec(block, lambda i: (0, i, 0))
        return pl.BlockSpec(block, lambda i: (i, 0))

    return pl.pallas_call(
        kernel,
        grid=(steps,),
        in_specs=[spec(array.shape, block) for array, block in operands],
        out_specs=[spec(shape, block) for _, shape, block in outs],
        out_shape=[jax.ShapeDtypeStruct(shape, dtype) for dtype, shape, _ in outs],
        scratch_shapes=[pltpu.VMEM(shape, dtype) for dtype, shape in scratch],
        compiler_params=pltpu.CompilerParams(vmem_limit_bytes=VMEM_LIMIT),
        cost_estimate=cost(us),
        name=kernel.__name__,
    )(*[array for array, _ in operands])


def per_device(
    frames_in, memory, counts, query_weight, key_weight, value_weight, out_weight, up_weight, down_weight,
    input_gain, middle_gain, output_gain, out_grad, memory_grad,
):
    slots, _, width = frames_in.shape
    ff = up_weight.shape[1]
    steps = slots // BLOCK
    total = slots * FRAMES
    parts = slots // PART
    tiles = slots // GROUP
    pick_query, pick_key, pick_carry, need, segment_of = tables()
    unpick_query, unpick_key, unpick_carry = (jnp.asarray(pick.T, BF) for pick in (pick_query, pick_key, pick_carry))
    pick_query, pick_key, pick_carry = (jnp.asarray(pick, BF) for pick in (pick_query, pick_key, pick_carry))
    need, segment_of = jnp.asarray(need), jnp.asarray(segment_of)
    input_gain, middle_gain, output_gain = (g.reshape(1, width) for g in (input_gain, middle_gain, output_gain))
    frames = jnp.transpose(frames_in, (1, 0, 2))
    pulls = jnp.transpose(out_grad, (1, 0, 2))
    segment = lax.axis_index("seg") * slots + jnp.arange(slots, dtype=jnp.int32)
    position = segment_position(counts[0], segment)
    halo = jnp.concatenate(
        [
            frames[:, slots - 2 :].reshape(CARRY_FRAMES, width),
            memory[slots - MEMS :],
            jnp.zeros((CARRY - CARRY_FRAMES - MEMS, width), BF),
        ],
        axis=0,
    )
    halo = shift(halo, "seg", 1)
    slab = (FRAMES, BLOCK, width)
    smem = pl.BlockSpec(memory_space=pltpu.SMEM)

    query_rows, key_rows, query, window = call(
        project_kernel,
        steps,
        [
            (frames, slab), (memory, (BLOCK, width)), (halo, None), (input_gain, None),
            (query_weight, None), (key_weight, None), (value_weight, None),
            (pick_query, None), (pick_key, None), (pick_carry, None),
        ],
        [
            (BF, (parts * PART_ROWS, width), (FULL, width)),
            (BF, (parts * (PART_ROWS + CARRY), width), (PARTS * (PART_ROWS + CARRY), width)),
            (BF, (tiles * TILE, width), (TILES, width)),
            (BF, (tiles * TILE, 2 * width), (TILES, 2 * width)),
        ],
        [(BF, (CARRY, width)), (BF, (CARRY, 2 * width))],
        8,
    )

    attended, soft, residual, slope, grad_combined, result, memory_out, grad_down, output_part = call(
        forward_kernel,
        steps,
        [
            (position, smem), (need, None), (segment_of, None), (unpick_query, None),
            (query, (TILES, width)), (window, (TILES, 2 * width)), (frames, slab), (pulls, slab),
            (out_weight, None), (up_weight, None), (down_weight, None), (middle_gain, None), (output_gain, None),
        ],
        [
            (BF, (parts * PART_ROWS, width), (FULL, width)),
            (BF, (tiles * PAIRS * TILE, 2 * TILE), (TILES * PAIRS, 2 * TILE)),
            (F32, (total, width), (ROWS, width)),
            (BF, (total, ff), (ROWS, ff)),
            (F32, (total, width), (ROWS, width)),
            (BF, (FRAMES, slots, width), slab),
            (BF, (slots, width), (BLOCK, width)),
            (BF, (ff, width), None),
            (F32, (1, width), None),
        ],
        [(BF, (width, PART_TILES)), (BF, (total, ff)), (BF, (total, width))],
        24,
    )

    down = Sum(grad_down, 2)
    down.start()

    grad_residual, grad_attended, grad_up_out, middle_part = call(
        backward_kernel,
        steps,
        [
            (slope, (ROWS, ff)), (grad_combined, (ROWS, width)), (residual, (ROWS, width)), (attended, (FULL, width)),
            (memory_grad, (BLOCK, width)), (out_weight, None), (up_weight, None), (down_weight, None), (middle_gain, None),
        ],
        [
            (F32, (total, width), (ROWS, width)),
            (BF, (parts * PART_ROWS, width), (FULL, width)),
            (BF, (width, ff + width), None),
            (F32, (1, width), None),
        ],
        [(BF, (total, ff)), (BF, (total, width)), (F32, (width, width))],
        16,
    )

    down.land()
    down.values, grad_attended = lax.optimization_barrier((down.values, grad_attended))
    up = Sum(grad_up_out, 0)
    up.start()
    down.start()

    grad_query_rows, grad_pair, grad_carry, grad_projections = call(
        attention_back_kernel,
        steps,
        [
            (pick_query, None), (unpick_query, None), (unpick_key, None),
            (query_rows, (FULL, width)), (key_rows, (PARTS * (PART_ROWS + CARRY), width)),
            (query, (TILES, width)), (window, (TILES, 2 * width)),
            (soft, (TILES * PAIRS, 2 * TILE)), (grad_attended, (FULL, width)),
        ],
        [
            (BF, (parts * PART_ROWS, width), (FULL, width)),
            (BF, (parts * PART_ROWS, 2 * width), (FULL, 2 * width)),
            (BF, (parts * CARRY, 2 * width), (PARTS * CARRY, 2 * width)),
            (BF, (width, 3 * width), None),
        ],
        [
            (BF, (width, PART_TILES)), (BF, (PART_TILES, 2 * width)), (F32, (width, width)), (F32, (width, 2 * width)),
        ],
        12,
    )

    projections = Sum(grad_projections, 2)
    down.land()
    up.land()
    down.values, up.values, projections.values, grad_carry = lax.optimization_barrier(
        (down.values, up.values, projections.values, grad_carry)
    )
    sent = projections.start()
    carry_next = shift(grad_carry[:CARRY], "seg", -1)
    sent = up.start(sent)
    sent = down.start(sent)

    grad_frames, grad_memory, input_part = call(
        projection_back_kernel,
        steps,
        [
            (unpick_carry, None), (grad_pair, (FULL, 2 * width)), (grad_carry, None), (carry_next, None),
            (grad_query_rows, (FULL, width)), (frames, slab), (grad_residual, (ROWS, width)),
            (query_weight, None), (key_weight, None), (value_weight, None), (input_gain, None),
        ],
        [
            (F32, (FRAMES, slots, width), slab),
            (BF, (slots, width), (BLOCK, width)),
            (F32, (1, width), None),
        ],
        [],
        8,
    )
    result = jnp.transpose(result, (1, 0, 2))
    grad_frames = jnp.transpose(grad_frames, (1, 0, 2))

    gains = jnp.concatenate([input_part, middle_part, output_part], axis=1)
    projections.land(sent)
    sent = projections.start(sent)
    up.land(sent, gains)
    projections.row = None
    order = (up, down, projections)
    turn = 0
    while not all(one.complete() for one in order):
        one = order[turn % 3]
        turn += 1
        if one.complete():
            continue
        if turn > 1:
            one.land(sent)
        if one is projections and one.done == len(one.steps):
            one.row = gains
        if not one.complete():
            sent = one.start(sent)
    gains = projections.row
    (grad_down,) = finish(down, [width])
    grad_up, grad_out = finish(up, [ff, width])
    grad_query, grad_key, grad_value = finish(projections, [width] * 3)
    gains = gains.reshape(3, width)
    return (
        result, memory_out, grad_frames, grad_memory,
        grad_query, grad_key, grad_value, grad_out, grad_up, grad_down,
        gains[0], gains[1], gains[2],
    )


def solution(mesh):
    rows = P(("grp", "seg"), None, None)
    singles = P(("grp", "seg"), None)
    return jax.shard_map(
        per_device,
        mesh=mesh,
        in_specs=(rows, singles, P("grp", None)) + (P(),) * 9 + (rows, singles),
        out_specs=(rows, singles, rows, singles) + (P(),) * 9,
        check_vma=False,
    )
```

```python
import jax
import jax.numpy as jnp
import numpy as np
from jax import lax
from jax.experimental import pallas as pl
from jax.experimental.pallas import tpu as pltpu
from jax.sharding import PartitionSpec as P

HEADS = 8
HDIM = 64
SEGLEN = 16
RIGHT = 4
LEFT = 30
MEMS = 4
FRAMES = RIGHT + SEGLEN

GROUP = 4
TILE = 128
PART = 8
PART_FRAMES = FRAMES * PART
PART_ROWS = PART_FRAMES + 2 * PART
PART_TILES = PART // GROUP * TILE
CARRY = 48
CARRY_FRAMES = 2 * FRAMES
BLOCK = 16
PARTS = BLOCK // PART
ROWS = BLOCK * FRAMES
FULL = PARTS * PART_ROWS
TILES = PARTS * PART_TILES
PAIRS = HEADS // 2
PAIR = 2 * HDIM

EPSILON = 1e-05
MASKED_SCORE = -1e30
FAR = 1 << 20

BF = jnp.bfloat16
F32 = jnp.float32
VMEM_LIMIT = 60 * 1024 * 1024
FINISH_VMEM = 60 * 1024 * 1024


def dot(a, b):
    return lax.dot_general(a, b, (((1,), (0,)), ((), ())), preferred_element_type=F32)


def dot_back(a, b):
    return lax.dot_general(a, b, (((1,), (1,)), ((), ())), preferred_element_type=F32)


def dot_outer(a, b):
    return lax.dot_general(a, b, (((0,), (0,)), ((), ())), preferred_element_type=F32)


def tables():
    pick_query = np.zeros((PART_TILES, PART_ROWS), np.float32)
    pick_key = np.zeros((PART_TILES, PART_ROWS + CARRY), np.float32)
    pick_carry = np.zeros((CARRY, PART_ROWS), np.float32)
    for group in range(PART // GROUP):
        for row in range(GROUP * FRAMES):
            segment = group * GROUP + row // FRAMES
            pick_query[group * TILE + row, row % FRAMES * PART + segment] = 1
        for row in range(GROUP):
            pick_query[group * TILE + GROUP * FRAMES + row, PART_FRAMES + group * GROUP + row] = 1
        for row in range((GROUP + 2) * FRAMES):
            segment, frame = group * GROUP - 2 + row // FRAMES, row % FRAMES
            column = frame * PART + segment if segment >= 0 else PART_ROWS + frame * 2 + segment + 2
            pick_key[group * TILE + row, column] = 1
        for row in range(GROUP + MEMS):
            segment = group * GROUP - MEMS + row
            column = PART_FRAMES + segment if segment >= 0 else PART_ROWS + CARRY_FRAMES + segment + MEMS
            pick_key[group * TILE + (GROUP + 2) * FRAMES + row, column] = 1
    for frame in range(FRAMES):
        for back in range(2):
            pick_carry[frame * 2 + back, frame * PART + PART - 2 + back] = 1
    for back in range(MEMS):
        pick_carry[CARRY_FRAMES + back, PART_FRAMES + PART - MEMS + back] = 1
    row = np.arange(TILE)
    is_summary = (row >= GROUP * FRAMES) & (row < GROUP * FRAMES + GROUP)
    segment = np.where(is_summary, row - GROUP * FRAMES, np.where(row < GROUP * FRAMES, row // FRAMES, 0))
    is_memory = row >= (GROUP + 2) * FRAMES
    key_segment = np.where(is_memory, row - (GROUP + 2) * FRAMES - MEMS, row // FRAMES - 2)
    within = row % FRAMES
    is_right = ~is_memory & (within < RIGHT)
    behind = segment[None, :] - key_segment[:, None]
    late = (within >= RIGHT + 2 * SEGLEN - LEFT)[:, None]
    frame_ok = (behind == 0) | (~is_right[:, None] & ((behind == 1) | ((behind == 2) & late)))
    memory_ok = (behind >= 1) & (behind <= MEMS) & ~is_summary[None, :]
    need = np.where(np.where(is_memory[:, None], memory_ok, frame_ok), behind, FAR).astype(np.int32)
    segment_of = np.ascontiguousarray(np.broadcast_to(segment[None, :], (TILE, TILE))).astype(np.int32)
    return pick_query, pick_key, pick_carry, need, segment_of


def row_stats(values):
    centered = values - jnp.mean(values, axis=-1, keepdims=True)
    spread = jnp.mean(centered * centered, axis=-1, keepdims=True)
    scale = lax.rsqrt(spread + EPSILON)
    return centered * scale, scale


def norm_back(unit, scale, gain, gradient):
    gained = gradient * gain
    along = jnp.mean(gained * unit, axis=-1, keepdims=True)
    grad = scale * (gained - jnp.mean(gained, axis=-1, keepdims=True) - unit * along)
    return grad, jnp.sum(gradient * unit, axis=0, keepdims=True)


def by_part(slabs):
    frames, _, width = slabs.shape
    return [slabs[:, p * PART : (p + 1) * PART].reshape(frames * PART, width) for p in range(PARTS)]


def by_frame(parts):
    return jnp.concatenate([part.reshape(FRAMES, PART, part.shape[1]) for part in parts], axis=1)


def project_kernel(
    frames, memory, gain, query_w, key_w, value_w, pick_query, pick_key, pick_carry,
    query_rows, key_rows, query, window,
    carry_rows, carry_pair,
):
    step = pl.program_id(0)

    @pl.when(step == 0)
    def _():
        carry_rows[...] = jnp.zeros_like(carry_rows)
        carry_pair[...] = jnp.zeros_like(carry_pair)

    memories = memory[...].astype(F32)
    asks, keys = [], []
    for p, part in enumerate(by_part(frames[...].astype(F32))):
        unit, _ = row_stats(part)
        normed = unit * gain[...]
        mean = normed[RIGHT * PART : (RIGHT + 1) * PART]
        for f in range(RIGHT + 1, FRAMES):
            mean = mean + normed[f * PART : (f + 1) * PART]
        mean = mean * (1.0 / SEGLEN)
        blank = jnp.zeros_like(mean)
        asks += [normed, mean, blank]
        keys += [normed, memories[p * PART : (p + 1) * PART], blank]
    asks = jnp.concatenate(asks, axis=0).astype(BF)
    keys = jnp.concatenate(keys, axis=0).astype(BF)
    query_rows[...] = asks
    asked = (dot(asks, query_w[...]) * 0.125).astype(BF)
    pair = jnp.concatenate([dot(keys, key_w[...]), dot(keys, value_w[...])], axis=1).astype(BF)
    for p in range(PARTS):
        part = slice(p * PART_ROWS, (p + 1) * PART_ROWS)
        at = p * (PART_ROWS + CARRY)
        key_rows[at : at + PART_ROWS] = keys[part]
        key_rows[at + PART_ROWS : at + PART_ROWS + CARRY] = carry_rows[...]
        query[p * PART_TILES : (p + 1) * PART_TILES] = dot(pick_query[...], asked[part]).astype(BF)
        both = jnp.concatenate([pair[part], carry_pair[...]], axis=0)
        window[p * PART_TILES : (p + 1) * PART_TILES] = dot(pick_key[...], both).astype(BF)
        carry_rows[...] = dot(pick_carry[...], keys[part]).astype(BF)
        carry_pair[...] = dot(pick_carry[...], pair[part]).astype(BF)


def halo_kernel(halo, gain, key_w, value_w, pick_late, key_rows_in, window_in, key_rows, window):
    raw = halo[...].astype(F32)
    unit, _ = row_stats(raw)
    is_frame = lax.broadcasted_iota(jnp.int32, raw.shape, 0) < CARRY_FRAMES
    carried = jnp.where(is_frame, unit * gain[...], raw).astype(BF)
    key_rows[:PART_ROWS] = key_rows_in[:PART_ROWS]
    key_rows[PART_ROWS:] = carried
    pair = jnp.concatenate([dot(carried, key_w[...]), dot(carried, value_w[...])], axis=1).astype(BF)
    window[...] = (window_in[...].astype(F32) + dot(pick_late[...], pair)).astype(BF)


def two_heads(rows):
    low = lax.broadcasted_iota(jnp.int32, (1, PAIR), 1) < HDIM
    wide = rows.astype(F32)
    return jnp.concatenate([jnp.where(low, wide, 0.0), jnp.where(low, 0.0, wide)], axis=0).astype(BF)


def of_two_heads(columns):
    return jnp.concatenate([columns[:HDIM, :TILE], columns[HDIM:, TILE:]], axis=0).astype(BF)


def gelu_parts(lifted):
    bell = jnp.exp(lifted * lifted * -0.5) * 0.3989422804014327
    share = 0.5 + 0.5 * lax.erf(lifted * 0.7071067811865476)
    return lifted * share, share + lifted * bell


def forward_kernel(
    core, position, need, segment_of, unpick_query, query, window, frames, out_grad,
    middle_gain, output_gain, out_w, up_w, down_w,
    attended, soft, residual_out, slope, grad_combined_out, result, memory_out, down_keep, down_send, grad_gain,
    turned, hidden, grad_ff_rows,
):
    step = pl.program_id(0)
    steps = pl.num_programs(0)
    width = out_w.shape[0]
    ff = up_w.shape[1]
    for p in range(PARTS):
        for g in range(PART // GROUP):
            tile = p * (PART // GROUP) + g
            first = step * BLOCK + tile * GROUP
            column = segment_of[...]
            at = jnp.where(
                column < 2,
                jnp.where(column == 0, position[first], position[first + 1]),
                jnp.where(column == 2, position[first + 2], position[first + 3]),
            )
            bias = jnp.where(at >= need[...], 0.0, MASKED_SCORE)
            bias = jnp.concatenate([bias, bias], axis=1)
            rows = slice(tile * TILE, (tile + 1) * TILE)
            for h in range(PAIRS):
                lanes = slice(h * PAIR, (h + 1) * PAIR)
                keys = window[rows, lanes]
                values = window[rows, width + h * PAIR : width + (h + 1) * PAIR]
                scores = dot_back(keys, two_heads(query[rows, lanes])) + bias
                powers = jnp.exp(scores - jnp.max(scores, axis=0, keepdims=True))
                soft_low = (powers * (1.0 / jnp.sum(powers, axis=0, keepdims=True))).astype(BF)
                spot = (tile * PAIRS + h) * TILE
                soft[spot : spot + TILE] = soft_low
                turned[lanes, g * TILE : (g + 1) * TILE] = of_two_heads(dot_outer(values, soft_low))
        attended[p * PART_ROWS : (p + 1) * PART_ROWS] = dot_back(unpick_query[...], turned[...]).astype(BF)
    branch = dot(attended[...], out_w[...])
    own = frames[...].astype(F32)
    residual, memory_rows = [], []
    for p, part in enumerate(by_part(own)):
        at = p * PART_ROWS
        residual.append(part + branch[at : at + PART_FRAMES])
        memory_rows.append(branch[at + PART_FRAMES : at + PART_FRAMES + PART])
    memory_out[...] = jnp.concatenate(memory_rows, axis=0).astype(BF)
    residual = jnp.concatenate(residual, axis=0)
    residual_out[...] = residual
    unit, _ = row_stats(residual)
    middle = (unit * middle_gain[...]).astype(BF)
    span = pl.ds(pl.multiple_of(step * ROWS, ROWS), ROWS)
    for c in range(ff // width):
        columns = slice(c * width, (c + 1) * width)
        part, turn = gelu_parts(dot(middle, up_w[:, columns]))
        part = part.astype(BF)
        hidden[span, columns] = part
        slope[:, columns] = turn.astype(BF)
    combined = residual + dot(hidden[span], down_w[...])
    unit, scale = row_stats(combined)
    final = unit * output_gain[...]
    result[...] = by_frame([final[p * PART_FRAMES : (p + 1) * PART_FRAMES] for p in range(PARTS)]).astype(BF)
    pulled = jnp.concatenate(by_part(out_grad[...].astype(F32)), axis=0)
    grad_combined, gain_part = norm_back(unit, scale, output_gain[...], pulled)
    grad_combined_out[...] = grad_combined
    grad_ff_rows[span] = grad_combined.astype(BF)

    @pl.when(step == 0)
    def _():
        grad_gain[...] = gain_part

    @pl.when(step > 0)
    def _():
        grad_gain[...] += gain_part

    @pl.when(step == steps - 1)
    def _():
        for half, out in ((core[0], down_keep), (1 - core[0], down_send)):
            for c in range(ff // width // 2):
                columns = pl.ds(pl.multiple_of(half * (ff // 2) + c * width, width), width)
                out[c * width : (c + 1) * width] = dot_outer(hidden[:, columns], grad_ff_rows[...]).astype(BF)


def backward_kernel(
    core, slope, grad_combined, residual, attended, memory_grad, middle_gain, out_w, up_w, down_w,
    grad_residual_out, grad_attended, up_keep, up_send, grad_gain,
    lifted, middle_rows, out_sum,
):
    step = pl.program_id(0)
    steps = pl.num_programs(0)
    width = out_w.shape[0]
    ff = up_w.shape[1]
    span = pl.ds(pl.multiple_of(step * ROWS, ROWS), ROWS)
    unit, scale = row_stats(residual[...])
    middle_rows[span] = (unit * middle_gain[...]).astype(BF)
    grad_combined_rows = grad_combined[...]
    grad_ff = grad_combined_rows.astype(BF)
    for c in range(ff // width):
        columns = slice(c * width, (c + 1) * width)
        part = (dot_back(grad_ff, down_w[columns]) * slope[:, columns].astype(F32)).astype(BF)
        lifted[span, columns] = part
    grad_middle = dot_back(lifted[span], up_w[...])
    grad_norm, gain_part = norm_back(unit, scale, middle_gain[...], grad_middle)
    grad_residual = grad_combined_rows + grad_norm
    grad_residual_out[...] = grad_residual
    memory_rows = memory_grad[...].astype(F32)
    blank = jnp.zeros((PART, width), F32)
    grad_branch = []
    for p in range(PARTS):
        grad_branch += [grad_residual[p * PART_FRAMES : (p + 1) * PART_FRAMES], memory_rows[p * PART : (p + 1) * PART], blank]
    grad_branch = jnp.concatenate(grad_branch, axis=0).astype(BF)
    grad_attended[...] = dot_back(grad_branch, out_w[...]).astype(BF)
    out_part = dot_outer(attended[...], grad_branch)

    @pl.when(step == 0)
    def _():
        grad_gain[...] = gain_part
        out_sum[...] = out_part

    @pl.when(step > 0)
    def _():
        grad_gain[...] += gain_part
        out_sum[...] += out_part

    @pl.when(step == steps - 1)
    def _():
        for half, out in ((core[0], up_keep), (1 - core[0], up_send)):
            rows = pl.ds(pl.multiple_of(half * (width // 2), width // 2), width // 2)
            out[:, :ff] = dot_outer(middle_rows[:, rows], lifted[...]).astype(BF)
            out[:, ff:] = out_sum[rows].astype(BF)


def attention_back_kernel(
    core, pick_query, unpick_query, unpick_key, query_rows, key_rows, query, window, soft, grad_attended,
    grad_query_rows, grad_pair, grad_carry, projections_keep, projections_send,
    turned, grad_window, both_rows, query_sum, pair_sum,
):
    step = pl.program_id(0)
    steps = pl.num_programs(0)
    width = query.shape[1]

    @pl.when(step == 0)
    def _():
        query_sum[...] = jnp.zeros_like(query_sum)
        pair_sum[...] = jnp.zeros_like(pair_sum)

    for p in range(PARTS):
        pulled = dot(pick_query[...], grad_attended[p * PART_ROWS : (p + 1) * PART_ROWS]).astype(BF)
        for g in range(PART // GROUP):
            tile = p * (PART // GROUP) + g
            rows = slice(tile * TILE, (tile + 1) * TILE)
            spread = slice(g * TILE, (g + 1) * TILE)
            for h in range(PAIRS):
                lanes = slice(h * PAIR, (h + 1) * PAIR)
                value_lanes = slice(width + h * PAIR, width + (h + 1) * PAIR)
                keys = window[rows, lanes]
                values = window[rows, value_lanes]
                asks = two_heads(query[rows, lanes])
                grads = two_heads(pulled[spread, lanes])
                spot = (tile * PAIRS + h) * TILE
                soft_low = soft[spot : spot + TILE]
                soft_wide = soft_low.astype(F32)
                weighted = dot_back(values, grads) * soft_wide
                grad_scores = (weighted - soft_wide * jnp.sum(weighted, axis=0, keepdims=True)).astype(BF)
                grad_window[spread, lanes] = dot(grad_scores, asks).astype(BF)
                grad_window[spread, value_lanes] = dot(soft_low, grads).astype(BF)
                turned[lanes, spread] = of_two_heads(dot_outer(keys, grad_scores))
        part = slice(p * PART_ROWS, (p + 1) * PART_ROWS)
        grad_asks = dot_back(unpick_query[...], turned[...]).astype(BF)
        grad_query_rows[part] = grad_asks
        both = dot(unpick_key[...], grad_window[...]).astype(BF)
        grad_pair[part] = both[:PART_ROWS]
        grad_carry[p * CARRY : (p + 1) * CARRY] = both[PART_ROWS:]
        both_rows[p * (PART_ROWS + CARRY) : (p + 1) * (PART_ROWS + CARRY)] = both
    query_sum[...] += dot_outer(query_rows[...], grad_query_rows[...])
    pair_sum[...] += dot_outer(key_rows[...], both_rows[...])

    @pl.when(step == steps - 1)
    def _():
        for half, out in ((core[0], projections_keep), (1 - core[0], projections_send)):
            rows = pl.ds(pl.multiple_of(half * (width // 2), width // 2), width // 2)
            out[:, :width] = (query_sum[rows] * 0.125).astype(BF)
            out[:, width:] = pair_sum[rows].astype(BF)


def projection_back_kernel(
    unpick_carry, grad_pair, grad_carry, carry_next, grad_query_rows, frames, grad_residual, query_w, key_w, value_w, gain,
    grad_frames, grad_memory, grad_gain,
):
    step = pl.program_id(0)
    steps = pl.num_programs(0)
    width = query_w.shape[0]
    pairs = []
    for p in range(PARTS):
        after = step * PARTS + p + 1
        inside = jnp.minimum(after, steps * PARTS - 1)
        late = grad_carry[pl.ds(pl.multiple_of(inside * CARRY, CARRY), CARRY)]
        if p == PARTS - 1:
            late = jnp.where(step == steps - 1, carry_next[...].astype(F32), late.astype(F32)).astype(BF)
        pairs.append(grad_pair[p * PART_ROWS : (p + 1) * PART_ROWS].astype(F32) + dot(unpick_carry[...], late))
    pair = jnp.concatenate(pairs, axis=0).astype(BF)
    query_back = dot_back(grad_query_rows[...], query_w[...]) * 0.125
    key_back = dot_back(pair[:, :width], key_w[...]) + dot_back(pair[:, width:], value_w[...])
    memory_rows, results = [], []
    gain_part = jnp.zeros((1, width), F32)
    for p, part in enumerate(by_part(frames[...].astype(F32))):
        at = p * PART_ROWS
        end = at + PART_FRAMES
        memory_rows.append(key_back[end : end + PART])
        own = query_back[at:end] + key_back[at:end]
        share = query_back[end : end + PART] * (1.0 / SEGLEN)
        share = jnp.concatenate([jnp.zeros((RIGHT * PART, width), F32)] + [share] * SEGLEN, axis=0)
        unit, scale = row_stats(part)
        grad_norm, more = norm_back(unit, scale, gain[...], own + share)
        gain_part = gain_part + more
        results.append(grad_residual[p * PART_FRAMES : (p + 1) * PART_FRAMES] + grad_norm)
    grad_frames[...] = by_frame(results)
    grad_memory[...] = jnp.concatenate(memory_rows, axis=0).astype(BF)

    @pl.when(step == 0)
    def _():
        grad_gain[...] = gain_part

    @pl.when(step > 0)
    def _():
        grad_gain[...] += gain_part


def cost(us):
    return pl.CostEstimate(flops=int(us * 1e9), bytes_accessed=int(us * 1e5), transcendentals=0)


def segment_position(counts_row, segment):
    order = jnp.arange(counts_row.shape[0], dtype=jnp.int32)
    starts = jnp.sum(jnp.where(order[None, :] < order[:, None], counts_row[None, :], 0), axis=1)
    first = jnp.max(jnp.where(starts[None, :] <= segment[:, None], starts[None, :], 0), axis=1)
    return segment - first


def shift(values, axis, by):
    size = lax.axis_size(axis)
    return lax.ppermute(values, axis, [(i, (i + by) % size) for i in range(size)])


def axis_bits(axis):
    return [1 << i for i in range(lax.axis_size(axis).bit_length() - 1)]


def chain(turn):
    bits = axis_bits("seg")
    few = min(3, len(bits))

    def turned(by):
        by = by % max(1, few)
        return bits[by:few] + bits[:by] + bits[few:]

    return ["grp"] + list(zip(turned(turn), turned(turn + 1)))


def side(stage):
    if stage == "grp":
        return lax.axis_index("grp")
    place = lax.axis_index("seg")
    return jnp.where(lax.axis_index("grp") == 0, place // stage[0] % 2, place // stage[1] % 2)


def swap(values, stage):
    if stage == "grp":
        return lax.ppermute(values, "grp", [(0, 1), (1, 0)])
    size = lax.axis_size("seg")
    pairs = [(core * size + i, core * size + (i ^ stage[core])) for core in range(2) for i in range(size)]
    return lax.ppermute(values, ("grp", "seg"), pairs)


def split_sum(total):
    high = total.astype(BF)
    return high, (total - high.astype(F32)).astype(BF)


class Sum:
    def __init__(self, keep, send, turn):
        self.values = keep
        self.first = send
        self.turn = turn
        self.steps = chain(turn)
        self.done = 0
        self.row = None

    def start(self, tie=None):
        count = len(self.steps)
        if self.done < count:
            stage = self.steps[self.done]
            if self.done == 0:
                send = self.first
            else:
                rows = self.values.shape[0] // 2
                own = side(stage)
                self.values, send = (
                    lax.dynamic_slice_in_dim(self.values, half * rows, rows, 0) for half in (own, 1 - own)
                )
        else:
            stage = self.steps[2 * count - 1 - self.done]
            send = self.values
            if self.row is not None:
                blank = jnp.zeros((6, self.row.shape[1]), BF)
                send = jnp.concatenate([send, *split_sum(self.row), blank], axis=0)
        if tie is not None:
            send, _ = lax.optimization_barrier((send, tie))
        self.arriving = swap(send, stage)
        return send

    def land(self, *ties):
        count = len(self.steps)
        other = lax.optimization_barrier((self.arriving,) + ties)[0] if ties else self.arriving
        if self.done < count:
            self.values = (self.values.astype(F32) + other.astype(F32)).astype(self.values.dtype)
        else:
            rows = self.values.shape[0]
            if self.row is not None:
                high, low = split_sum(self.row)
                theirs = other[rows : rows + 1].astype(F32) + other[rows + 1 : rows + 2].astype(F32)
                self.row = high.astype(F32) + low.astype(F32) + theirs
                other = other[:rows]
            if self.done < 2 * count - 1:
                self.values = jnp.concatenate([self.values, other], axis=0)
            else:
                self.other = other
        self.done += 1

    def complete(self):
        return self.done == 2 * len(self.steps)


def shares(turn, core, place):
    found = []
    for which in range(2):
        share = 0
        for stage in chain(turn)[1:]:
            share = share * 2 + place // stage[which] % 2
        found.append(share)
    return jnp.where(core == 0, found[0], found[1]), jnp.where(core == 0, found[1], found[0])


def finish(total, widths, device):
    own, other = total.values, total.other
    half = own.shape[0]
    count = lax.axis_size("seg")
    rows = half // count
    cuts = np.cumsum(widths)[:-1].tolist()
    if rows % 16:
        index = jnp.arange(count, dtype=jnp.int32)
        mine, theirs = (
            jnp.take(part.reshape(count, rows, -1), index ^ share, axis=0).reshape(half, -1)
            for part, share in zip((own, other[:half]), shares(total.turn, device[0], device[1]))
        )
        whole = jnp.where(device[0] == 0, jnp.concatenate([mine, theirs]), jnp.concatenate([theirs, mine]))
        return jnp.split(whole.astype(F32), cuts, axis=1)
    halves = 2

    def kernel(device_ref, own_ref, other_ref, *outs):
        step = pl.program_id(0)
        mine = (step // halves) == device_ref[0]
        own_share, other_share = shares(total.turn, device_ref[0], device_ref[1])

        def fill(source, share):
            for j in range(count // halves):
                piece = (step % halves * (count // halves) + j) ^ share
                block = source[pl.ds(pl.multiple_of(piece * rows, rows), rows)].astype(F32)
                at = 0
                for out in outs:
                    out[j * rows : (j + 1) * rows] = block[:, at : at + out.shape[1]]
                    at += out.shape[1]

        @pl.when(mine)
        def _():
            fill(own_ref, own_share)

        @pl.when(jnp.logical_not(mine))
        def _():
            fill(other_ref, other_share)

    return pl.pallas_call(
        kernel,
        grid=(2 * halves,),
        in_specs=[pl.BlockSpec(memory_space=pltpu.SMEM)] + [pl.BlockSpec(part.shape, lambda i: (0, 0)) for part in (own, other)],
        out_specs=[pl.BlockSpec((half // halves, w), lambda i: (i, 0)) for w in widths],
        out_shape=[jax.ShapeDtypeStruct((2 * half, w), F32) for w in widths],
        compiler_params=pltpu.CompilerParams(vmem_limit_bytes=FINISH_VMEM),
        cost_estimate=cost(3),
        name="finish",
    )(device, own, other)


def call(kernel, steps, operands, outs, scratch, us, aliases=None):
    def spec(shape, block):
        if isinstance(block, pl.BlockSpec):
            return block
        if block is None:
            return pl.BlockSpec(shape, lambda i: (0,) * len(shape))
        if len(block) == 3:
            return pl.BlockSpec(block, lambda i: (0, i, 0))
        return pl.BlockSpec(block, lambda i: (i, 0))

    return pl.pallas_call(
        kernel,
        grid=(steps,),
        in_specs=[spec(array.shape, block) for array, block in operands],
        out_specs=[spec(shape, block) for _, shape, block in outs],
        out_shape=[jax.ShapeDtypeStruct(shape, dtype) for dtype, shape, _ in outs],
        scratch_shapes=[pltpu.VMEM(shape, dtype) for dtype, shape in scratch],
        input_output_aliases=aliases or {},
        compiler_params=pltpu.CompilerParams(vmem_limit_bytes=VMEM_LIMIT),
        cost_estimate=cost(us),
        name=kernel.__name__,
    )(*[array for array, _ in operands])


def per_device(
    frames_in, memory, counts, query_weight, key_weight, value_weight, out_weight, up_weight, down_weight,
    input_gain, middle_gain, output_gain, out_grad, memory_grad,
):
    slots, _, width = frames_in.shape
    ff = up_weight.shape[1]
    steps = slots // BLOCK
    total = slots * FRAMES
    parts = slots // PART
    tiles = slots // GROUP
    pick_query, pick_key, pick_carry, need, segment_of = tables()
    unpick_query, unpick_key, unpick_carry = (jnp.asarray(pick.T, BF) for pick in (pick_query, pick_key, pick_carry))
    pick_late = jnp.asarray(pick_key[:, PART_ROWS:], BF)
    pick_query, pick_key, pick_carry = (jnp.asarray(pick, BF) for pick in (pick_query, pick_key, pick_carry))
    device = jnp.stack([lax.axis_index("grp"), lax.axis_index("seg")]).astype(jnp.int32)
    need, segment_of = jnp.asarray(need), jnp.asarray(segment_of)
    input_gain, middle_gain, output_gain = (g.reshape(1, width) for g in (input_gain, middle_gain, output_gain))
    frames = jnp.transpose(frames_in, (1, 0, 2))
    pulls = jnp.transpose(out_grad, (1, 0, 2))
    segment = lax.axis_index("seg") * slots + jnp.arange(slots, dtype=jnp.int32)
    position = segment_position(counts[0], segment)
    halo = jnp.concatenate(
        [
            frames[:, slots - 2 :].reshape(CARRY_FRAMES, width),
            memory[slots - MEMS :],
            jnp.zeros((CARRY - CARRY_FRAMES - MEMS, width), BF),
        ],
        axis=0,
    )
    halo = shift(halo, "seg", 1)
    slab = (FRAMES, BLOCK, width)
    smem = pl.BlockSpec(memory_space=pltpu.SMEM)

    query_rows, key_rows, query, window = call(
        project_kernel,
        steps,
        [
            (frames, slab), (memory, (BLOCK, width)), (input_gain, None),
            (query_weight, None), (key_weight, None), (value_weight, None),
            (pick_query, None), (pick_key, None), (pick_carry, None),
        ],
        [
            (BF, (parts * PART_ROWS, width), (FULL, width)),
            (BF, (parts * (PART_ROWS + CARRY), width), (PARTS * (PART_ROWS + CARRY), width)),
            (BF, (tiles * TILE, width), (TILES, width)),
            (BF, (tiles * TILE, 2 * width), (TILES, 2 * width)),
        ],
        [(BF, (CARRY, width)), (BF, (CARRY, 2 * width))],
        10,
    )

    key_block = pl.BlockSpec((PART_ROWS + CARRY, width), lambda i: (0, 0))
    window_block = pl.BlockSpec((PART_TILES, 2 * width), lambda i: (0, 0))
    key_rows, window = call(
        halo_kernel,
        1,
        [
            (halo, None), (input_gain, None), (key_weight, None), (value_weight, None), (pick_late, None),
            (key_rows, key_block), (window, window_block),
        ],
        [(BF, key_rows.shape, key_block), (BF, window.shape, window_block)],
        [],
        2,
        {5: 0, 6: 1},
    )

    attended, soft, residual, slope, grad_combined, result, memory_out, keep, send, output_part = call(
        forward_kernel,
        steps,
        [
            (device, smem), (position, smem), (need, None), (segment_of, None), (unpick_query, None),
            (query, (TILES, width)), (window, (TILES, 2 * width)), (frames, slab), (pulls, slab),
            (middle_gain, None), (output_gain, None), (out_weight, None), (up_weight, None), (down_weight, None),
        ],
        [
            (BF, (parts * PART_ROWS, width), (FULL, width)),
            (BF, (tiles * PAIRS * TILE, 2 * TILE), (TILES * PAIRS, 2 * TILE)),
            (F32, (total, width), (ROWS, width)),
            (BF, (total, ff), (ROWS, ff)),
            (F32, (total, width), (ROWS, width)),
            (BF, (FRAMES, slots, width), slab),
            (BF, (slots, width), (BLOCK, width)),
            (BF, (ff // 2, width), None),
            (BF, (ff // 2, width), None),
            (F32, (1, width), None),
        ],
        [(BF, (width, PART_TILES)), (BF, (total, ff)), (BF, (total, width))],
        24,
    )

    down = Sum(keep, send, 2)
    down.start()

    grad_residual, grad_attended, keep, send, middle_part = call(
        backward_kernel,
        steps,
        [
            (device, smem), (slope, (ROWS, ff)), (grad_combined, (ROWS, width)), (residual, (ROWS, width)), (attended, (FULL, width)),
            (memory_grad, (BLOCK, width)), (middle_gain, None), (out_weight, None), (up_weight, None), (down_weight, None),
        ],
        [
            (F32, (total, width), (ROWS, width)),
            (BF, (parts * PART_ROWS, width), (FULL, width)),
            (BF, (width // 2, ff + width), None),
            (BF, (width // 2, ff + width), None),
            (F32, (1, width), None),
        ],
        [(BF, (total, ff)), (BF, (total, width)), (F32, (width, width))],
        16,
    )

    down.land()
    down.values, grad_attended = lax.optimization_barrier((down.values, grad_attended))
    up = Sum(keep, send, 0)
    up.start()
    down.start()

    grad_query_rows, grad_pair, grad_carry, keep, send = call(
        attention_back_kernel,
        steps,
        [
            (device, smem), (pick_query, None), (unpick_query, None), (unpick_key, None),
            (query_rows, (FULL, width)), (key_rows, (PARTS * (PART_ROWS + CARRY), width)),
            (query, (TILES, width)), (window, (TILES, 2 * width)),
            (soft, (TILES * PAIRS, 2 * TILE)), (grad_attended, (FULL, width)),
        ],
        [
            (BF, (parts * PART_ROWS, width), (FULL, width)),
            (BF, (parts * PART_ROWS, 2 * width), (FULL, 2 * width)),
            (BF, (parts * CARRY, 2 * width), (PARTS * CARRY, 2 * width)),
            (BF, (width // 2, 3 * width), None),
            (BF, (width // 2, 3 * width), None),
        ],
        [
            (BF, (width, PART_TILES)), (BF, (PART_TILES, 2 * width)), (BF, (PARTS * (PART_ROWS + CARRY), 2 * width)),
            (F32, (width, width)), (F32, (width, 2 * width)),
        ],
        12,
    )

    down.land()
    up.land()
    down.values, up.values, keep, send, grad_carry = lax.optimization_barrier(
        (down.values, up.values, keep, send, grad_carry)
    )
    projections = Sum(keep, send, 0)
    sent = projections.start()
    carry_next = shift(grad_carry[:CARRY], "seg", -1)
    sent = up.start(sent)
    sent = down.start(sent)
    grad_frames, grad_memory, input_part = call(
        projection_back_kernel,
        steps,
        [
            (unpick_carry, None), (grad_pair, (FULL, 2 * width)), (grad_carry, None), (carry_next, None),
            (grad_query_rows, (FULL, width)), (frames, slab), (grad_residual, (ROWS, width)),
            (query_weight, None), (key_weight, None), (value_weight, None), (input_gain, None),
        ],
        [
            (F32, (FRAMES, slots, width), slab),
            (BF, (slots, width), (BLOCK, width)),
            (F32, (1, width), None),
        ],
        [],
        8,
    )
    result = jnp.transpose(result, (1, 0, 2))
    grad_frames = jnp.transpose(grad_frames, (1, 0, 2))

    gains = jnp.concatenate([input_part, middle_part, output_part], axis=1)
    projections.land(sent)
    sent = projections.start(sent)
    up.land(sent, gains)
    projections.row = None
    order = (up, down, projections)
    cuts = {up: [ff, width], down: [width], projections: [width] * 3}
    ready = {}
    held = ()
    turn = 0
    while not all(one.complete() for one in order):
        one = order[turn % 3]
        turn += 1
        if one.complete():
            continue
        if turn > 1:
            one.land(sent, *(held if one is projections else ()))
        if one is projections and one.done == len(one.steps):
            one.row = gains
        if one.complete():
            ready[one] = finish(one, cuts[one], device)
            held = held + tuple(ready[one])
        else:
            sent = one.start(sent)
    gains = projections.row
    (grad_down,) = ready[down]
    grad_up, grad_out = ready[up]
    grad_query, grad_key, grad_value = ready[projections]
    gains = gains.reshape(3, width)
    return (
        result, memory_out, grad_frames, grad_memory,
        grad_query, grad_key, grad_value, grad_out, grad_up, grad_down,
        gains[0], gains[1], gains[2],
    )


def solution(mesh):
    rows = P(("grp", "seg"), None, None)
    singles = P(("grp", "seg"), None)
    return jax.shard_map(
        per_device,
        mesh=mesh,
        in_specs=(rows, singles, P("grp", None)) + (P(),) * 9 + (rows, singles),
        out_specs=(rows, singles, rows, singles) + (P(),) * 9,
        check_vma=False,
    )
```

```python
import jax
import jax.numpy as jnp
import numpy as np
from jax import lax
from jax.experimental import pallas as pl
from jax.experimental.pallas import tpu as pltpu
from jax.sharding import PartitionSpec as P

HEADS = 8
HDIM = 64
SEGLEN = 16
RIGHT = 4
LEFT = 30
MEMS = 4
FRAMES = RIGHT + SEGLEN

GROUP = 4
TILE = 128
PART = 8
PART_FRAMES = FRAMES * PART
PART_ROWS = PART_FRAMES + 2 * PART
PART_TILES = PART // GROUP * TILE
CARRY = 48
CARRY_FRAMES = 2 * FRAMES
BLOCK = 16
PARTS = BLOCK // PART
ROWS = BLOCK * FRAMES
FULL = PARTS * PART_ROWS
TILES = PARTS * PART_TILES
PAIRS = HEADS // 2
PAIR = 2 * HDIM

EPSILON = 1e-05
MASKED_SCORE = -1e30
FAR = 1 << 20

BF = jnp.bfloat16
F32 = jnp.float32
VMEM_LIMIT = 60 * 1024 * 1024
FINISH_VMEM = 60 * 1024 * 1024


def dot(a, b):
    return lax.dot_general(a, b, (((1,), (0,)), ((), ())), preferred_element_type=F32)


def dot_back(a, b):
    return lax.dot_general(a, b, (((1,), (1,)), ((), ())), preferred_element_type=F32)


def dot_outer(a, b):
    return lax.dot_general(a, b, (((0,), (0,)), ((), ())), preferred_element_type=F32)


def tables():
    pick_query = np.zeros((PART_TILES, PART_ROWS), np.float32)
    pick_key = np.zeros((PART_TILES, PART_ROWS + CARRY), np.float32)
    pick_carry = np.zeros((CARRY, PART_ROWS), np.float32)
    for group in range(PART // GROUP):
        for row in range(GROUP * FRAMES):
            segment = group * GROUP + row // FRAMES
            pick_query[group * TILE + row, row % FRAMES * PART + segment] = 1
        for row in range(GROUP):
            pick_query[group * TILE + GROUP * FRAMES + row, PART_FRAMES + group * GROUP + row] = 1
        for row in range((GROUP + 2) * FRAMES):
            segment, frame = group * GROUP - 2 + row // FRAMES, row % FRAMES
            column = frame * PART + segment if segment >= 0 else PART_ROWS + frame * 2 + segment + 2
            pick_key[group * TILE + row, column] = 1
        for row in range(GROUP + MEMS):
            segment = group * GROUP - MEMS + row
            column = PART_FRAMES + segment if segment >= 0 else PART_ROWS + CARRY_FRAMES + segment + MEMS
            pick_key[group * TILE + (GROUP + 2) * FRAMES + row, column] = 1
    for frame in range(FRAMES):
        for back in range(2):
            pick_carry[frame * 2 + back, frame * PART + PART - 2 + back] = 1
    for back in range(MEMS):
        pick_carry[CARRY_FRAMES + back, PART_FRAMES + PART - MEMS + back] = 1
    row = np.arange(TILE)
    is_summary = (row >= GROUP * FRAMES) & (row < GROUP * FRAMES + GROUP)
    segment = np.where(is_summary, row - GROUP * FRAMES, np.where(row < GROUP * FRAMES, row // FRAMES, 0))
    is_memory = row >= (GROUP + 2) * FRAMES
    key_segment = np.where(is_memory, row - (GROUP + 2) * FRAMES - MEMS, row // FRAMES - 2)
    within = row % FRAMES
    is_right = ~is_memory & (within < RIGHT)
    behind = segment[None, :] - key_segment[:, None]
    late = (within >= RIGHT + 2 * SEGLEN - LEFT)[:, None]
    frame_ok = (behind == 0) | (~is_right[:, None] & ((behind == 1) | ((behind == 2) & late)))
    memory_ok = (behind >= 1) & (behind <= MEMS) & ~is_summary[None, :]
    need = np.where(np.where(is_memory[:, None], memory_ok, frame_ok), behind, FAR).astype(np.int32)
    segment_of = np.ascontiguousarray(np.broadcast_to(segment[None, :], (TILE, TILE))).astype(np.int32)
    return pick_query, pick_key, pick_carry, need, segment_of


def row_stats(values):
    centered = values - jnp.mean(values, axis=-1, keepdims=True)
    spread = jnp.mean(centered * centered, axis=-1, keepdims=True)
    scale = lax.rsqrt(spread + EPSILON)
    return centered * scale, scale


def norm_back(unit, scale, gain, gradient):
    gained = gradient * gain
    along = jnp.mean(gained * unit, axis=-1, keepdims=True)
    grad = scale * (gained - jnp.mean(gained, axis=-1, keepdims=True) - unit * along)
    return grad, jnp.sum(gradient * unit, axis=0, keepdims=True)


def by_part(slabs):
    frames, _, width = slabs.shape
    return [slabs[:, p * PART : (p + 1) * PART].reshape(frames * PART, width) for p in range(PARTS)]


def by_frame(parts):
    return jnp.concatenate([part.reshape(FRAMES, PART, part.shape[1]) for part in parts], axis=1)


def project_kernel(
    frames, memory, gain, query_w, key_w, value_w, pick_query, pick_key, pick_carry,
    query_rows, key_rows, query, window,
    carry_rows, carry_pair,
):
    step = pl.program_id(0)

    @pl.when(step == 0)
    def _():
        carry_rows[...] = jnp.zeros_like(carry_rows)
        carry_pair[...] = jnp.zeros_like(carry_pair)

    memories = memory[...].astype(F32)
    asks, keys = [], []
    for p, part in enumerate(by_part(frames[...].astype(F32))):
        unit, _ = row_stats(part)
        normed = unit * gain[...]
        mean = normed[RIGHT * PART : (RIGHT + 1) * PART]
        for f in range(RIGHT + 1, FRAMES):
            mean = mean + normed[f * PART : (f + 1) * PART]
        mean = mean * (1.0 / SEGLEN)
        blank = jnp.zeros_like(mean)
        asks += [normed, mean, blank]
        keys += [normed, memories[p * PART : (p + 1) * PART], blank]
    asks = jnp.concatenate(asks, axis=0).astype(BF)
    keys = jnp.concatenate(keys, axis=0).astype(BF)
    query_rows[...] = asks
    asked = (dot(asks, query_w[...]) * 0.125).astype(BF)
    pair = jnp.concatenate([dot(keys, key_w[...]), dot(keys, value_w[...])], axis=1).astype(BF)
    for p in range(PARTS):
        part = slice(p * PART_ROWS, (p + 1) * PART_ROWS)
        at = p * (PART_ROWS + CARRY)
        key_rows[at : at + PART_ROWS] = keys[part]
        key_rows[at + PART_ROWS : at + PART_ROWS + CARRY] = carry_rows[...]
        query[p * PART_TILES : (p + 1) * PART_TILES] = dot(pick_query[...], asked[part]).astype(BF)
        both = jnp.concatenate([pair[part], carry_pair[...]], axis=0)
        window[p * PART_TILES : (p + 1) * PART_TILES] = dot(pick_key[...], both).astype(BF)
        carry_rows[...] = dot(pick_carry[...], keys[part]).astype(BF)
        carry_pair[...] = dot(pick_carry[...], pair[part]).astype(BF)


def halo_kernel(halo, gain, key_w, value_w, pick_carry, pick_late, key_rows_in, window_in, key_rows, window):
    slabs = halo[...].astype(F32)
    unit, _ = row_stats(slabs[:FRAMES].reshape(PART_FRAMES, slabs.shape[2]))
    rows = jnp.concatenate([unit * gain[...], slabs[FRAMES], jnp.zeros_like(slabs[FRAMES])], axis=0).astype(BF)
    carried = dot(pick_carry[...], rows).astype(BF)
    key_rows[:PART_ROWS] = key_rows_in[:PART_ROWS]
    key_rows[PART_ROWS:] = carried
    pair = jnp.concatenate([dot(carried, key_w[...]), dot(carried, value_w[...])], axis=1).astype(BF)
    window[...] = (window_in[...].astype(F32) + dot(pick_late[...], pair)).astype(BF)


def two_heads(rows):
    low = lax.broadcasted_iota(jnp.int32, (1, PAIR), 1) < HDIM
    wide = rows.astype(F32)
    return jnp.concatenate([jnp.where(low, wide, 0.0), jnp.where(low, 0.0, wide)], axis=0).astype(BF)


def of_two_heads(columns):
    return jnp.concatenate([columns[:HDIM, :TILE], columns[HDIM:, TILE:]], axis=0).astype(BF)


def gelu_parts(lifted):
    bell = jnp.exp(lifted * lifted * -0.5) * 0.3989422804014327
    share = 0.5 + 0.5 * lax.erf(lifted * 0.7071067811865476)
    return lifted * share, share + lifted * bell


def forward_kernel(
    core, position, need, segment_of, unpick_query, query, window, frames, out_grad,
    middle_gain, output_gain, out_w, up_w, down_w,
    attended, soft, residual_out, slope, grad_combined_out, result, memory_out, down_keep, down_send, grad_gain,
    turned, hidden, grad_ff_rows,
):
    step = pl.program_id(0)
    steps = pl.num_programs(0)
    width = out_w.shape[0]
    ff = up_w.shape[1]
    for p in range(PARTS):
        for g in range(PART // GROUP):
            tile = p * (PART // GROUP) + g
            first = step * BLOCK + tile * GROUP
            column = segment_of[...]
            at = jnp.where(
                column < 2,
                jnp.where(column == 0, position[first], position[first + 1]),
                jnp.where(column == 2, position[first + 2], position[first + 3]),
            )
            bias = jnp.where(at >= need[...], 0.0, MASKED_SCORE)
            bias = jnp.concatenate([bias, bias], axis=1)
            rows = slice(tile * TILE, (tile + 1) * TILE)
            for h in range(PAIRS):
                lanes = slice(h * PAIR, (h + 1) * PAIR)
                keys = window[rows, lanes]
                values = window[rows, width + h * PAIR : width + (h + 1) * PAIR]
                scores = dot_back(keys, two_heads(query[rows, lanes])) + bias
                powers = jnp.exp(scores - jnp.max(scores, axis=0, keepdims=True))
                soft_low = (powers * (1.0 / jnp.sum(powers, axis=0, keepdims=True))).astype(BF)
                spot = (tile * PAIRS + h) * TILE
                soft[spot : spot + TILE] = soft_low
                turned[lanes, g * TILE : (g + 1) * TILE] = of_two_heads(dot_outer(values, soft_low))
        attended[p * PART_ROWS : (p + 1) * PART_ROWS] = dot_back(unpick_query[...], turned[...]).astype(BF)
    branch = dot(attended[...], out_w[...])
    own = frames[...].astype(F32)
    residual, memory_rows = [], []
    for p, part in enumerate(by_part(own)):
        at = p * PART_ROWS
        residual.append(part + branch[at : at + PART_FRAMES])
        memory_rows.append(branch[at + PART_FRAMES : at + PART_FRAMES + PART])
    memory_out[...] = jnp.concatenate(memory_rows, axis=0).astype(BF)
    residual = jnp.concatenate(residual, axis=0)
    residual_out[...] = residual
    unit, _ = row_stats(residual)
    middle = (unit * middle_gain[...]).astype(BF)
    span = pl.ds(pl.multiple_of(step * ROWS, ROWS), ROWS)
    for c in range(ff // width):
        columns = slice(c * width, (c + 1) * width)
        part, turn = gelu_parts(dot(middle, up_w[:, columns]))
        part = part.astype(BF)
        hidden[span, columns] = part
        slope[:, columns] = turn.astype(BF)
    combined = residual + dot(hidden[span], down_w[...])
    unit, scale = row_stats(combined)
    final = unit * output_gain[...]
    result[...] = by_frame([final[p * PART_FRAMES : (p + 1) * PART_FRAMES] for p in range(PARTS)]).astype(BF)
    pulled = jnp.concatenate(by_part(out_grad[...].astype(F32)), axis=0)
    grad_combined, gain_part = norm_back(unit, scale, output_gain[...], pulled)
    grad_ff = grad_combined.astype(BF)
    grad_combined_out[...] = grad_ff
    grad_ff_rows[span] = grad_ff

    @pl.when(step == 0)
    def _():
        grad_gain[...] = gain_part

    @pl.when(step > 0)
    def _():
        grad_gain[...] += gain_part

    @pl.when(step == steps - 1)
    def _():
        for half, out in ((core[0], down_keep), (1 - core[0], down_send)):
            for c in range(ff // width // 2):
                columns = pl.ds(pl.multiple_of(half * (ff // 2) + c * width, width), width)
                out[c * width : (c + 1) * width] = dot_outer(hidden[:, columns], grad_ff_rows[...]).astype(BF)


def backward_kernel(
    core, slope, grad_combined, residual, attended, memory_grad, middle_gain, out_w, up_w, down_w,
    grad_residual_out, grad_attended, up_keep, up_send, grad_gain,
    lifted, middle_rows, out_sum,
):
    step = pl.program_id(0)
    steps = pl.num_programs(0)
    width = out_w.shape[0]
    ff = up_w.shape[1]
    span = pl.ds(pl.multiple_of(step * ROWS, ROWS), ROWS)
    unit, scale = row_stats(residual[...])
    middle_rows[span] = (unit * middle_gain[...]).astype(BF)
    grad_ff = grad_combined[...]
    for c in range(ff // width):
        columns = slice(c * width, (c + 1) * width)
        part = (dot_back(grad_ff, down_w[columns]) * slope[:, columns].astype(F32)).astype(BF)
        lifted[span, columns] = part
    grad_middle = dot_back(lifted[span], up_w[...])
    grad_norm, gain_part = norm_back(unit, scale, middle_gain[...], grad_middle)
    grad_residual = grad_ff.astype(F32) + grad_norm
    grad_residual_out[...] = grad_residual.astype(BF)
    memory_rows = memory_grad[...].astype(F32)
    blank = jnp.zeros((PART, width), F32)
    grad_branch = []
    for p in range(PARTS):
        grad_branch += [grad_residual[p * PART_FRAMES : (p + 1) * PART_FRAMES], memory_rows[p * PART : (p + 1) * PART], blank]
    grad_branch = jnp.concatenate(grad_branch, axis=0).astype(BF)
    grad_attended[...] = dot_back(grad_branch, out_w[...]).astype(BF)
    out_part = dot_outer(attended[...], grad_branch)

    @pl.when(step == 0)
    def _():
        grad_gain[...] = gain_part
        out_sum[...] = out_part

    @pl.when(step > 0)
    def _():
        grad_gain[...] += gain_part
        out_sum[...] += out_part

    @pl.when(step == steps - 1)
    def _():
        for half, out in ((core[0], up_keep), (1 - core[0], up_send)):
            rows = pl.ds(pl.multiple_of(half * (width // 2), width // 2), width // 2)
            out[:, :ff] = dot_outer(middle_rows[:, rows], lifted[...]).astype(BF)
            out[:, ff:] = out_sum[rows].astype(BF)


def store_first(out, values, step):
    @pl.when(step == 0)
    def _():
        out[...] = values


def attention_back_kernel(
    core, pick_query, unpick_query, unpick_key, query_rows, key_rows, query, window, soft, grad_attended,
    grad_query_rows, grad_pair, grad_carry, first_carry, projections_keep, projections_send,
    turned, grad_window, both_rows, query_sum, pair_sum,
):
    step = pl.program_id(0)
    steps = pl.num_programs(0)
    width = query.shape[1]

    @pl.when(step == 0)
    def _():
        query_sum[...] = jnp.zeros_like(query_sum)
        pair_sum[...] = jnp.zeros_like(pair_sum)

    for p in range(PARTS):
        pulled = dot(pick_query[...], grad_attended[p * PART_ROWS : (p + 1) * PART_ROWS]).astype(BF)
        for g in range(PART // GROUP):
            tile = p * (PART // GROUP) + g
            rows = slice(tile * TILE, (tile + 1) * TILE)
            spread = slice(g * TILE, (g + 1) * TILE)
            for h in range(PAIRS):
                lanes = slice(h * PAIR, (h + 1) * PAIR)
                value_lanes = slice(width + h * PAIR, width + (h + 1) * PAIR)
                keys = window[rows, lanes]
                values = window[rows, value_lanes]
                asks = two_heads(query[rows, lanes])
                grads = two_heads(pulled[spread, lanes])
                spot = (tile * PAIRS + h) * TILE
                soft_low = soft[spot : spot + TILE]
                soft_wide = soft_low.astype(F32)
                weighted = dot_back(values, grads) * soft_wide
                grad_scores = (weighted - soft_wide * jnp.sum(weighted, axis=0, keepdims=True)).astype(BF)
                grad_window[spread, lanes] = dot(grad_scores, asks).astype(BF)
                grad_window[spread, value_lanes] = dot(soft_low, grads).astype(BF)
                turned[lanes, spread] = of_two_heads(dot_outer(keys, grad_scores))
        part = slice(p * PART_ROWS, (p + 1) * PART_ROWS)
        grad_asks = dot_back(unpick_query[...], turned[...]).astype(BF)
        grad_query_rows[part] = grad_asks
        both = dot(unpick_key[...], grad_window[...]).astype(BF)
        grad_pair[part] = both[:PART_ROWS]
        grad_carry[p * CARRY : (p + 1) * CARRY] = both[PART_ROWS:]
        if p == 0:
            store_first(first_carry, both[PART_ROWS:], step)
        both_rows[p * (PART_ROWS + CARRY) : (p + 1) * (PART_ROWS + CARRY)] = both
    query_sum[...] += dot_outer(query_rows[...], grad_query_rows[...])
    pair_sum[...] += dot_outer(key_rows[...], both_rows[...])

    @pl.when(step == steps - 1)
    def _():
        for half, out in ((core[0], projections_keep), (1 - core[0], projections_send)):
            rows = pl.ds(pl.multiple_of(half * (width // 2), width // 2), width // 2)
            out[:, :width] = (query_sum[rows] * 0.125).astype(BF)
            out[:, width:] = pair_sum[rows].astype(BF)


def projection_back_kernel(
    unpick_carry, grad_pair, grad_carry, carry_next, grad_query_rows, frames, grad_residual, query_w, key_w, value_w, gain,
    grad_frames, grad_memory, grad_gain,
):
    step = pl.program_id(0)
    steps = pl.num_programs(0)
    width = query_w.shape[0]
    pairs = []
    for p in range(PARTS):
        after = step * PARTS + p + 1
        inside = jnp.minimum(after, steps * PARTS - 1)
        late = grad_carry[pl.ds(pl.multiple_of(inside * CARRY, CARRY), CARRY)]
        if p == PARTS - 1:
            late = jnp.where(step == steps - 1, carry_next[...].astype(F32), late.astype(F32)).astype(BF)
        pairs.append(grad_pair[p * PART_ROWS : (p + 1) * PART_ROWS].astype(F32) + dot(unpick_carry[...], late))
    pair = jnp.concatenate(pairs, axis=0).astype(BF)
    query_back = dot_back(grad_query_rows[...], query_w[...]) * 0.125
    key_back = dot_back(pair[:, :width], key_w[...]) + dot_back(pair[:, width:], value_w[...])
    memory_rows, results = [], []
    gain_part = jnp.zeros((1, width), F32)
    for p, part in enumerate(by_part(frames[...].astype(F32))):
        at = p * PART_ROWS
        end = at + PART_FRAMES
        memory_rows.append(key_back[end : end + PART])
        own = query_back[at:end] + key_back[at:end]
        share = query_back[end : end + PART] * (1.0 / SEGLEN)
        share = jnp.concatenate([jnp.zeros((RIGHT * PART, width), F32)] + [share] * SEGLEN, axis=0)
        unit, scale = row_stats(part)
        grad_norm, more = norm_back(unit, scale, gain[...], own + share)
        gain_part = gain_part + more
        results.append(grad_residual[p * PART_FRAMES : (p + 1) * PART_FRAMES].astype(F32) + grad_norm)
    grad_frames[...] = by_frame(results)
    grad_memory[...] = jnp.concatenate(memory_rows, axis=0).astype(BF)

    @pl.when(step == 0)
    def _():
        grad_gain[...] = gain_part

    @pl.when(step > 0)
    def _():
        grad_gain[...] += gain_part


def cost(us):
    return pl.CostEstimate(flops=int(us * 1e9), bytes_accessed=int(us * 1e5), transcendentals=0)


def segment_position(counts_row, segment):
    order = jnp.arange(counts_row.shape[0], dtype=jnp.int32)
    starts = jnp.sum(jnp.where(order[None, :] < order[:, None], counts_row[None, :], 0), axis=1)
    first = jnp.max(jnp.where(starts[None, :] <= segment[:, None], starts[None, :], 0), axis=1)
    return segment - first


def shift(values, axis, by):
    size = lax.axis_size(axis)
    return lax.ppermute(values, axis, [(i, (i + by) % size) for i in range(size)])


def axis_bits(axis):
    return [1 << i for i in range(lax.axis_size(axis).bit_length() - 1)]


def chain(turn):
    bits = axis_bits("seg")
    few = min(3, len(bits))

    def turned(by):
        by = by % max(1, few)
        return bits[by:few] + bits[:by] + bits[few:]

    return ["grp"] + list(zip(turned(turn), turned(turn + 1)))


def side(stage):
    if stage == "grp":
        return lax.axis_index("grp")
    place = lax.axis_index("seg")
    return jnp.where(lax.axis_index("grp") == 0, place // stage[0] % 2, place // stage[1] % 2)


def swap(values, stage):
    if stage == "grp":
        return lax.ppermute(values, "grp", [(0, 1), (1, 0)])
    size = lax.axis_size("seg")
    pairs = [(core * size + i, core * size + (i ^ stage[core])) for core in range(2) for i in range(size)]
    return lax.ppermute(values, ("grp", "seg"), pairs)


def split_sum(total):
    high = total.astype(BF)
    return high, (total - high.astype(F32)).astype(BF)


class Sum:
    def __init__(self, keep, send, turn):
        self.values = keep
        self.first = send
        self.turn = turn
        self.steps = chain(turn)
        self.done = 0
        self.row = None

    def start(self, tie=None):
        count = len(self.steps)
        if self.done < count:
            stage = self.steps[self.done]
            if self.done == 0:
                send = self.first
            else:
                rows = self.values.shape[0] // 2
                own = side(stage)
                self.values, send = (
                    lax.dynamic_slice_in_dim(self.values, half * rows, rows, 0) for half in (own, 1 - own)
                )
        else:
            stage = self.steps[2 * count - 1 - self.done]
            send = self.values
            if self.row is not None:
                blank = jnp.zeros((6, self.row.shape[1]), BF)
                send = jnp.concatenate([send, *split_sum(self.row), blank], axis=0)
        if tie is not None:
            send, _ = lax.optimization_barrier((send, tie))
        self.arriving = swap(send, stage)
        return send

    def land(self, *ties):
        count = len(self.steps)
        other = lax.optimization_barrier((self.arriving,) + ties)[0] if ties else self.arriving
        if self.done < count:
            self.values = (self.values.astype(F32) + other.astype(F32)).astype(self.values.dtype)
        else:
            rows = self.values.shape[0]
            if self.row is not None:
                high, low = split_sum(self.row)
                theirs = other[rows : rows + 1].astype(F32) + other[rows + 1 : rows + 2].astype(F32)
                self.row = high.astype(F32) + low.astype(F32) + theirs
                other = other[:rows]
            if self.done < 2 * count - 1:
                self.values = jnp.concatenate([self.values, other], axis=0)
            else:
                self.other = other
        self.done += 1

    def complete(self):
        return self.done == 2 * len(self.steps)


def shares(turn, core, place):
    found = []
    for which in range(2):
        share = 0
        for stage in chain(turn)[1:]:
            share = share * 2 + place // stage[which] % 2
        found.append(share)
    return jnp.where(core == 0, found[0], found[1]), jnp.where(core == 0, found[1], found[0])


def finish(total, widths, device):
    own, other = total.values, total.other
    half = own.shape[0]
    count = lax.axis_size("seg")
    rows = half // count
    cuts = np.cumsum(widths)[:-1].tolist()
    if rows % 16:
        index = jnp.arange(count, dtype=jnp.int32)
        mine, theirs = (
            jnp.take(part.reshape(count, rows, -1), index ^ share, axis=0).reshape(half, -1)
            for part, share in zip((own, other[:half]), shares(total.turn, device[0], device[1]))
        )
        whole = jnp.where(device[0] == 0, jnp.concatenate([mine, theirs]), jnp.concatenate([theirs, mine]))
        return jnp.split(whole.astype(F32), cuts, axis=1)
    halves = 2

    def kernel(device_ref, own_ref, other_ref, *outs):
        step = pl.program_id(0)
        mine = (step // halves) == device_ref[0]
        own_share, other_share = shares(total.turn, device_ref[0], device_ref[1])

        def fill(source, share):
            for j in range(count // halves):
                piece = (step % halves * (count // halves) + j) ^ share
                block = source[pl.ds(pl.multiple_of(piece * rows, rows), rows)].astype(F32)
                at = 0
                for out in outs:
                    out[j * rows : (j + 1) * rows] = block[:, at : at + out.shape[1]]
                    at += out.shape[1]

        @pl.when(mine)
        def _():
            fill(own_ref, own_share)

        @pl.when(jnp.logical_not(mine))
        def _():
            fill(other_ref, other_share)

    return pl.pallas_call(
        kernel,
        grid=(2 * halves,),
        in_specs=[pl.BlockSpec(memory_space=pltpu.SMEM)] + [pl.BlockSpec(part.shape, lambda i: (0, 0)) for part in (own, other)],
        out_specs=[pl.BlockSpec((half // halves, w), lambda i: (i, 0)) for w in widths],
        out_shape=[jax.ShapeDtypeStruct((2 * half, w), F32) for w in widths],
        compiler_params=pltpu.CompilerParams(vmem_limit_bytes=FINISH_VMEM),
        cost_estimate=cost(3),
        name="finish",
    )(device, own, other)


def call(kernel, steps, operands, outs, scratch, us, aliases=None):
    def spec(shape, block):
        if isinstance(block, pl.BlockSpec):
            return block
        if block is None:
            return pl.BlockSpec(shape, lambda i: (0,) * len(shape))
        if len(block) == 3:
            return pl.BlockSpec(block, lambda i: (0, i, 0))
        return pl.BlockSpec(block, lambda i: (i, 0))

    return pl.pallas_call(
        kernel,
        grid=(steps,),
        in_specs=[spec(array.shape, block) for array, block in operands],
        out_specs=[spec(shape, block) for _, shape, block in outs],
        out_shape=[jax.ShapeDtypeStruct(shape, dtype) for dtype, shape, _ in outs],
        scratch_shapes=[pltpu.VMEM(shape, dtype) for dtype, shape in scratch],
        input_output_aliases=aliases or {},
        compiler_params=pltpu.CompilerParams(vmem_limit_bytes=VMEM_LIMIT),
        cost_estimate=cost(us),
        name=kernel.__name__,
    )(*[array for array, _ in operands])


def per_device(
    frames_in, memory, counts, query_weight, key_weight, value_weight, out_weight, up_weight, down_weight,
    input_gain, middle_gain, output_gain, out_grad, memory_grad,
):
    slots, _, width = frames_in.shape
    ff = up_weight.shape[1]
    steps = slots // BLOCK
    total = slots * FRAMES
    parts = slots // PART
    tiles = slots // GROUP
    pick_query, pick_key, pick_carry, need, segment_of = tables()
    unpick_query, unpick_key, unpick_carry = (jnp.asarray(pick.T, BF) for pick in (pick_query, pick_key, pick_carry))
    pick_late = jnp.asarray(pick_key[:, PART_ROWS:], BF)
    pick_query, pick_key, pick_carry = (jnp.asarray(pick, BF) for pick in (pick_query, pick_key, pick_carry))
    device = jnp.stack([lax.axis_index("grp"), lax.axis_index("seg")]).astype(jnp.int32)
    need, segment_of = jnp.asarray(need), jnp.asarray(segment_of)
    input_gain, middle_gain, output_gain = (g.reshape(1, width) for g in (input_gain, middle_gain, output_gain))
    frames = jnp.transpose(frames_in, (1, 0, 2))
    pulls = jnp.transpose(out_grad, (1, 0, 2))
    segment = lax.axis_index("seg") * slots + jnp.arange(slots, dtype=jnp.int32)
    position = segment_position(counts[0], segment)
    halo = jnp.concatenate([frames[:, slots - PART :], memory[None, slots - PART :]], axis=0)
    halo = shift(halo, "seg", 1)
    slab = (FRAMES, BLOCK, width)
    smem = pl.BlockSpec(memory_space=pltpu.SMEM)

    query_rows, key_rows, query, window = call(
        project_kernel,
        steps,
        [
            (frames, slab), (memory, (BLOCK, width)), (input_gain, None),
            (query_weight, None), (key_weight, None), (value_weight, None),
            (pick_query, None), (pick_key, None), (pick_carry, None),
        ],
        [
            (BF, (parts * PART_ROWS, width), (FULL, width)),
            (BF, (parts * (PART_ROWS + CARRY), width), (PARTS * (PART_ROWS + CARRY), width)),
            (BF, (tiles * TILE, width), (TILES, width)),
            (BF, (tiles * TILE, 2 * width), (TILES, 2 * width)),
        ],
        [(BF, (CARRY, width)), (BF, (CARRY, 2 * width))],
        10,
    )

    key_block = pl.BlockSpec((PART_ROWS + CARRY, width), lambda i: (0, 0))
    window_block = pl.BlockSpec((PART_TILES, 2 * width), lambda i: (0, 0))
    key_rows, window = call(
        halo_kernel,
        1,
        [
            (halo, pl.BlockSpec(halo.shape, lambda i: (0, 0, 0))), (input_gain, None), (key_weight, None), (value_weight, None),
            (pick_carry, None), (pick_late, None),
            (key_rows, key_block), (window, window_block),
        ],
        [(BF, key_rows.shape, key_block), (BF, window.shape, window_block)],
        [],
        2,
        {6: 0, 7: 1},
    )

    attended, soft, residual, slope, grad_combined, result, memory_out, keep, send, output_part = call(
        forward_kernel,
        steps,
        [
            (device, smem), (position, smem), (need, None), (segment_of, None), (unpick_query, None),
            (query, (TILES, width)), (window, (TILES, 2 * width)), (frames, slab), (pulls, slab),
            (middle_gain, None), (output_gain, None), (out_weight, None), (up_weight, None), (down_weight, None),
        ],
        [
            (BF, (parts * PART_ROWS, width), (FULL, width)),
            (BF, (tiles * PAIRS * TILE, 2 * TILE), (TILES * PAIRS, 2 * TILE)),
            (F32, (total, width), (ROWS, width)),
            (BF, (total, ff), (ROWS, ff)),
            (BF, (total, width), (ROWS, width)),
            (BF, (FRAMES, slots, width), slab),
            (BF, (slots, width), (BLOCK, width)),
            (BF, (ff // 2, width), None),
            (BF, (ff // 2, width), None),
            (F32, (1, width), None),
        ],
        [(BF, (width, PART_TILES)), (BF, (total, ff)), (BF, (total, width))],
        24,
    )

    down = Sum(keep, send, 2)
    down.start()

    grad_residual, grad_attended, keep, send, middle_part = call(
        backward_kernel,
        steps,
        [
            (device, smem), (slope, (ROWS, ff)), (grad_combined, (ROWS, width)), (residual, (ROWS, width)), (attended, (FULL, width)),
            (memory_grad, (BLOCK, width)), (middle_gain, None), (out_weight, None), (up_weight, None), (down_weight, None),
        ],
        [
            (BF, (total, width), (ROWS, width)),
            (BF, (parts * PART_ROWS, width), (FULL, width)),
            (BF, (width // 2, ff + width), None),
            (BF, (width // 2, ff + width), None),
            (F32, (1, width), None),
        ],
        [(BF, (total, ff)), (BF, (total, width)), (F32, (width, width))],
        16,
    )

    down.land()
    down.values, grad_attended = lax.optimization_barrier((down.values, grad_attended))
    up = Sum(keep, send, 0)
    up.start()
    down.start()

    grad_query_rows, grad_pair, grad_carry, first_carry, keep, send = call(
        attention_back_kernel,
        steps,
        [
            (device, smem), (pick_query, None), (unpick_query, None), (unpick_key, None),
            (query_rows, (FULL, width)), (key_rows, (PARTS * (PART_ROWS + CARRY), width)),
            (query, (TILES, width)), (window, (TILES, 2 * width)),
            (soft, (TILES * PAIRS, 2 * TILE)), (grad_attended, (FULL, width)),
        ],
        [
            (BF, (parts * PART_ROWS, width), (FULL, width)),
            (BF, (parts * PART_ROWS, 2 * width), (FULL, 2 * width)),
            (BF, (parts * CARRY, 2 * width), (PARTS * CARRY, 2 * width)),
            (BF, (CARRY, 2 * width), None),
            (BF, (width // 2, 3 * width), None),
            (BF, (width // 2, 3 * width), None),
        ],
        [
            (BF, (width, PART_TILES)), (BF, (PART_TILES, 2 * width)), (BF, (PARTS * (PART_ROWS + CARRY), 2 * width)),
            (F32, (width, width)), (F32, (width, 2 * width)),
        ],
        12,
    )

    projections = Sum(keep, send, 0)
    sent = projections.start()
    carry_next = shift(first_carry, "seg", -1)
    down.land()
    up.land()
    down.values, up.values, grad_pair = lax.optimization_barrier((down.values, up.values, grad_pair))
    sent = up.start(sent)
    sent = down.start(sent)
    projections.land(sent)
    sent = projections.start(sent)
    grad_pair, _ = lax.optimization_barrier((grad_pair, sent))

    grad_frames, grad_memory, input_part = call(
        projection_back_kernel,
        steps,
        [
            (unpick_carry, None), (grad_pair, (FULL, 2 * width)), (grad_carry, None), (carry_next, None),
            (grad_query_rows, (FULL, width)), (frames, slab), (grad_residual, (ROWS, width)),
            (query_weight, None), (key_weight, None), (value_weight, None), (input_gain, None),
        ],
        [
            (F32, (FRAMES, slots, width), slab),
            (BF, (slots, width), (BLOCK, width)),
            (F32, (1, width), None),
        ],
        [],
        8,
    )
    result = jnp.transpose(result, (1, 0, 2))
    grad_frames = jnp.transpose(grad_frames, (1, 0, 2))

    gains = jnp.concatenate([input_part, middle_part, output_part], axis=1)
    up.land(sent, gains)
    projections.row = None
    order = (up, down, projections)
    cuts = {up: [ff, width], down: [width], projections: [width] * 3}
    ready = {}
    held = ()
    turn = 0
    while not all(one.complete() for one in order):
        one = order[turn % 3]
        turn += 1
        if one.complete():
            continue
        if turn > 1:
            one.land(sent, *(held if one is projections else ()))
        if one is projections and one.done == len(one.steps):
            one.row = gains
        if one.complete():
            ready[one] = finish(one, cuts[one], device)
            held = held + tuple(ready[one])
        else:
            sent = one.start(sent)
    gains = projections.row
    (grad_down,) = ready[down]
    grad_up, grad_out = ready[up]
    grad_query, grad_key, grad_value = ready[projections]
    gains = gains.reshape(3, width)
    return (
        result, memory_out, grad_frames, grad_memory,
        grad_query, grad_key, grad_value, grad_out, grad_up, grad_down,
        gains[0], gains[1], gains[2],
    )


def solution(mesh):
    rows = P(("grp", "seg"), None, None)
    singles = P(("grp", "seg"), None)
    return jax.shard_map(
        per_device,
        mesh=mesh,
        in_specs=(rows, singles, P("grp", None)) + (P(),) * 9 + (rows, singles),
        out_specs=(rows, singles, rows, singles) + (P(),) * 9,
        check_vma=False,
    )
```

```python
import jax
import jax.numpy as jnp
import numpy as np
from jax import lax
from jax.experimental import pallas as pl
from jax.experimental.pallas import tpu as pltpu
from jax.sharding import PartitionSpec as P

HEADS = 8
HDIM = 64
SEGLEN = 16
RIGHT = 4
LEFT = 30
MEMS = 4
FRAMES = RIGHT + SEGLEN

GROUP = 4
TILE = 128
PART = 8
PART_FRAMES = FRAMES * PART
PART_ROWS = PART_FRAMES + 2 * PART
PART_TILES = PART // GROUP * TILE
CARRY = 48
CARRY_FRAMES = 2 * FRAMES
BLOCK = 16
PARTS = BLOCK // PART
ROWS = BLOCK * FRAMES
FULL = PARTS * PART_ROWS
TILES = PARTS * PART_TILES
PAIRS = HEADS // 2
PAIR = 2 * HDIM

EPSILON = 1e-05
MASKED_SCORE = -1e30
FAR = 1 << 20

BF = jnp.bfloat16
F32 = jnp.float32
VMEM_LIMIT = 60 * 1024 * 1024
FINISH_VMEM = 60 * 1024 * 1024


def dot(a, b):
    return lax.dot_general(a, b, (((1,), (0,)), ((), ())), preferred_element_type=F32)


def dot_back(a, b):
    return lax.dot_general(a, b, (((1,), (1,)), ((), ())), preferred_element_type=F32)


def dot_outer(a, b):
    return lax.dot_general(a, b, (((0,), (0,)), ((), ())), preferred_element_type=F32)


def tables():
    pick_query = np.zeros((PART_TILES, PART_ROWS), np.float32)
    pick_key = np.zeros((PART_TILES, PART_ROWS + CARRY), np.float32)
    pick_carry = np.zeros((CARRY, PART_ROWS), np.float32)
    for group in range(PART // GROUP):
        for row in range(GROUP * FRAMES):
            segment = group * GROUP + row // FRAMES
            pick_query[group * TILE + row, row % FRAMES * PART + segment] = 1
        for row in range(GROUP):
            pick_query[group * TILE + GROUP * FRAMES + row, PART_FRAMES + group * GROUP + row] = 1
        for row in range((GROUP + 2) * FRAMES):
            segment, frame = group * GROUP - 2 + row // FRAMES, row % FRAMES
            column = frame * PART + segment if segment >= 0 else PART_ROWS + frame * 2 + segment + 2
            pick_key[group * TILE + row, column] = 1
        for row in range(GROUP + MEMS):
            segment = group * GROUP - MEMS + row
            column = PART_FRAMES + segment if segment >= 0 else PART_ROWS + CARRY_FRAMES + segment + MEMS
            pick_key[group * TILE + (GROUP + 2) * FRAMES + row, column] = 1
    for frame in range(FRAMES):
        for back in range(2):
            pick_carry[frame * 2 + back, frame * PART + PART - 2 + back] = 1
    for back in range(MEMS):
        pick_carry[CARRY_FRAMES + back, PART_FRAMES + PART - MEMS + back] = 1
    row = np.arange(TILE)
    is_summary = (row >= GROUP * FRAMES) & (row < GROUP * FRAMES + GROUP)
    segment = np.where(is_summary, row - GROUP * FRAMES, np.where(row < GROUP * FRAMES, row // FRAMES, 0))
    is_memory = row >= (GROUP + 2) * FRAMES
    key_segment = np.where(is_memory, row - (GROUP + 2) * FRAMES - MEMS, row // FRAMES - 2)
    within = row % FRAMES
    is_right = ~is_memory & (within < RIGHT)
    behind = segment[None, :] - key_segment[:, None]
    late = (within >= RIGHT + 2 * SEGLEN - LEFT)[:, None]
    frame_ok = (behind == 0) | (~is_right[:, None] & ((behind == 1) | ((behind == 2) & late)))
    memory_ok = (behind >= 1) & (behind <= MEMS) & ~is_summary[None, :]
    need = np.where(np.where(is_memory[:, None], memory_ok, frame_ok), behind, FAR).astype(np.int32)
    segment_of = np.ascontiguousarray(np.broadcast_to(segment[None, :], (TILE, TILE))).astype(np.int32)
    return pick_query, pick_key, pick_carry, need, segment_of


def row_stats(values):
    centered = values - jnp.mean(values, axis=-1, keepdims=True)
    spread = jnp.mean(centered * centered, axis=-1, keepdims=True)
    scale = lax.rsqrt(spread + EPSILON)
    return centered * scale, scale


def norm_back(unit, scale, gain, gradient):
    gained = gradient * gain
    along = jnp.mean(gained * unit, axis=-1, keepdims=True)
    grad = scale * (gained - jnp.mean(gained, axis=-1, keepdims=True) - unit * along)
    return grad, jnp.sum(gradient * unit, axis=0, keepdims=True)


def by_part(slabs):
    frames, _, width = slabs.shape
    return [slabs[:, p * PART : (p + 1) * PART].reshape(frames * PART, width) for p in range(PARTS)]


def by_frame(parts):
    return jnp.concatenate([part.reshape(FRAMES, PART, part.shape[1]) for part in parts], axis=1)


def project_kernel(
    frames, memory, gain, query_w, key_w, value_w, pick_query, pick_key, pick_carry,
    query_rows, key_rows, query, window,
    carry_rows, carry_pair,
):
    step = pl.program_id(0)

    @pl.when(step == 0)
    def _():
        carry_rows[...] = jnp.zeros_like(carry_rows)
        carry_pair[...] = jnp.zeros_like(carry_pair)

    memories = memory[...].astype(F32)
    asks, keys = [], []
    for p, part in enumerate(by_part(frames[...].astype(F32))):
        unit, _ = row_stats(part)
        normed = unit * gain[...]
        mean = normed[RIGHT * PART : (RIGHT + 1) * PART]
        for f in range(RIGHT + 1, FRAMES):
            mean = mean + normed[f * PART : (f + 1) * PART]
        mean = mean * (1.0 / SEGLEN)
        blank = jnp.zeros_like(mean)
        asks += [normed, mean, blank]
        keys += [normed, memories[p * PART : (p + 1) * PART], blank]
    asks = jnp.concatenate(asks, axis=0).astype(BF)
    keys = jnp.concatenate(keys, axis=0).astype(BF)
    query_rows[...] = asks
    asked = (dot(asks, query_w[...]) * 0.125).astype(BF)
    pair = jnp.concatenate([dot(keys, key_w[...]), dot(keys, value_w[...])], axis=1).astype(BF)
    for p in range(PARTS):
        part = slice(p * PART_ROWS, (p + 1) * PART_ROWS)
        at = p * (PART_ROWS + CARRY)
        key_rows[at : at + PART_ROWS] = keys[part]
        key_rows[at + PART_ROWS : at + PART_ROWS + CARRY] = carry_rows[...]
        query[p * PART_TILES : (p + 1) * PART_TILES] = dot(pick_query[...], asked[part]).astype(BF)
        both = jnp.concatenate([pair[part], carry_pair[...]], axis=0)
        window[p * PART_TILES : (p + 1) * PART_TILES] = dot(pick_key[...], both).astype(BF)
        carry_rows[...] = dot(pick_carry[...], keys[part]).astype(BF)
        carry_pair[...] = dot(pick_carry[...], pair[part]).astype(BF)


def halo_kernel(halo, gain, key_w, value_w, pick_carry, pick_late, key_rows_in, window_in, key_rows, window):
    slabs = halo[...].astype(F32)
    unit, _ = row_stats(slabs[:FRAMES].reshape(PART_FRAMES, slabs.shape[2]))
    rows = jnp.concatenate([unit * gain[...], slabs[FRAMES], jnp.zeros_like(slabs[FRAMES])], axis=0).astype(BF)
    carried = dot(pick_carry[...], rows).astype(BF)
    key_rows[:PART_ROWS] = key_rows_in[:PART_ROWS]
    key_rows[PART_ROWS:] = carried
    pair = jnp.concatenate([dot(carried, key_w[...]), dot(carried, value_w[...])], axis=1).astype(BF)
    window[...] = (window_in[...].astype(F32) + dot(pick_late[...], pair)).astype(BF)


def two_heads(rows):
    low = lax.broadcasted_iota(jnp.int32, (1, PAIR), 1) < HDIM
    wide = rows.astype(F32)
    return jnp.concatenate([jnp.where(low, wide, 0.0), jnp.where(low, 0.0, wide)], axis=0).astype(BF)


def of_two_heads(columns):
    return jnp.concatenate([columns[:HDIM, :TILE], columns[HDIM:, TILE:]], axis=0).astype(BF)


def gelu_parts(lifted):
    bell = jnp.exp(lifted * lifted * -0.5) * 0.3989422804014327
    share = 0.5 + 0.5 * lax.erf(lifted * 0.7071067811865476)
    return lifted * share, share + lifted * bell


def forward_kernel(
    core, position, need, segment_of, unpick_query, query, window, frames, out_grad,
    middle_gain, output_gain, out_w, up_w, down_w,
    attended, soft, residual_out, slope, grad_combined_out, result, memory_out, down_keep, down_send, grad_gain,
    turned, hidden, grad_ff_rows,
):
    step = pl.program_id(0)
    steps = pl.num_programs(0)
    width = out_w.shape[0]
    ff = up_w.shape[1]
    for p in range(PARTS):
        for g in range(PART // GROUP):
            tile = p * (PART // GROUP) + g
            first = step * BLOCK + tile * GROUP
            column = segment_of[...]
            at = jnp.where(
                column < 2,
                jnp.where(column == 0, position[first], position[first + 1]),
                jnp.where(column == 2, position[first + 2], position[first + 3]),
            )
            bias = jnp.where(at >= need[...], 0.0, MASKED_SCORE)
            bias = jnp.concatenate([bias, bias], axis=1)
            rows = slice(tile * TILE, (tile + 1) * TILE)
            for h in range(PAIRS):
                lanes = slice(h * PAIR, (h + 1) * PAIR)
                keys = window[rows, lanes]
                values = window[rows, width + h * PAIR : width + (h + 1) * PAIR]
                scores = dot_back(keys, two_heads(query[rows, lanes])) + bias
                powers = jnp.exp(scores - jnp.max(scores, axis=0, keepdims=True))
                soft_low = (powers * (1.0 / jnp.sum(powers, axis=0, keepdims=True))).astype(BF)
                spot = (tile * PAIRS + h) * TILE
                soft[spot : spot + TILE] = soft_low
                turned[lanes, g * TILE : (g + 1) * TILE] = of_two_heads(dot_outer(values, soft_low))
        attended[p * PART_ROWS : (p + 1) * PART_ROWS] = dot_back(unpick_query[...], turned[...]).astype(BF)
    branch = dot(attended[...], out_w[...])
    own = frames[...].astype(F32)
    residual, memory_rows = [], []
    for p, part in enumerate(by_part(own)):
        at = p * PART_ROWS
        residual.append(part + branch[at : at + PART_FRAMES])
        memory_rows.append(branch[at + PART_FRAMES : at + PART_FRAMES + PART])
    memory_out[...] = jnp.concatenate(memory_rows, axis=0).astype(BF)
    residual = jnp.concatenate(residual, axis=0)
    residual_out[...] = residual.astype(BF)
    unit, _ = row_stats(residual)
    middle = (unit * middle_gain[...]).astype(BF)
    span = pl.ds(pl.multiple_of(step * ROWS, ROWS), ROWS)
    for c in range(ff // width):
        columns = slice(c * width, (c + 1) * width)
        part, turn = gelu_parts(dot(middle, up_w[:, columns]))
        part = part.astype(BF)
        hidden[span, columns] = part
        slope[:, columns] = turn.astype(BF)
    combined = residual + dot(hidden[span], down_w[...])
    unit, scale = row_stats(combined)
    final = unit * output_gain[...]
    result[...] = by_frame([final[p * PART_FRAMES : (p + 1) * PART_FRAMES] for p in range(PARTS)]).astype(BF)
    pulled = jnp.concatenate(by_part(out_grad[...].astype(F32)), axis=0)
    grad_combined, gain_part = norm_back(unit, scale, output_gain[...], pulled)
    grad_ff = grad_combined.astype(BF)
    grad_combined_out[...] = grad_ff
    grad_ff_rows[span] = grad_ff

    @pl.when(step == 0)
    def _():
        grad_gain[...] = gain_part

    @pl.when(step > 0)
    def _():
        grad_gain[...] += gain_part

    @pl.when(step == steps - 1)
    def _():
        for half, out in ((core[0], down_keep), (1 - core[0], down_send)):
            for c in range(ff // width // 2):
                columns = pl.ds(pl.multiple_of(half * (ff // 2) + c * width, width), width)
                out[c * width : (c + 1) * width] = dot_outer(hidden[:, columns], grad_ff_rows[...]).astype(BF)


def backward_kernel(
    core, slope, grad_combined, residual, attended, memory_grad, middle_gain, out_w, up_w, down_w,
    grad_residual_out, grad_attended, up_keep, up_send, grad_gain,
    lifted, middle_rows, out_sum,
):
    step = pl.program_id(0)
    steps = pl.num_programs(0)
    width = out_w.shape[0]
    ff = up_w.shape[1]
    span = pl.ds(pl.multiple_of(step * ROWS, ROWS), ROWS)
    unit, scale = row_stats(residual[...].astype(F32))
    middle_rows[span] = (unit * middle_gain[...]).astype(BF)
    grad_ff = grad_combined[...]
    for c in range(ff // width):
        columns = slice(c * width, (c + 1) * width)
        part = (dot_back(grad_ff, down_w[columns]) * slope[:, columns].astype(F32)).astype(BF)
        lifted[span, columns] = part
    grad_middle = dot_back(lifted[span], up_w[...])
    grad_norm, gain_part = norm_back(unit, scale, middle_gain[...], grad_middle)
    grad_residual = grad_ff.astype(F32) + grad_norm
    grad_residual_out[...] = grad_residual.astype(BF)
    memory_rows = memory_grad[...].astype(F32)
    blank = jnp.zeros((PART, width), F32)
    grad_branch = []
    for p in range(PARTS):
        grad_branch += [grad_residual[p * PART_FRAMES : (p + 1) * PART_FRAMES], memory_rows[p * PART : (p + 1) * PART], blank]
    grad_branch = jnp.concatenate(grad_branch, axis=0).astype(BF)
    grad_attended[...] = dot_back(grad_branch, out_w[...]).astype(BF)
    out_part = dot_outer(attended[...], grad_branch)

    @pl.when(step == 0)
    def _():
        grad_gain[...] = gain_part
        out_sum[...] = out_part

    @pl.when(step > 0)
    def _():
        grad_gain[...] += gain_part
        out_sum[...] += out_part

    @pl.when(step == steps - 1)
    def _():
        for half, out in ((core[0], up_keep), (1 - core[0], up_send)):
            rows = pl.ds(pl.multiple_of(half * (width // 2), width // 2), width // 2)
            out[:, :ff] = dot_outer(middle_rows[:, rows], lifted[...]).astype(BF)
            out[:, ff:] = out_sum[rows].astype(BF)


def store_first(out, values, step):
    @pl.when(step == 0)
    def _():
        out[...] = values


def attention_back_kernel(
    core, pick_query, unpick_query, unpick_key, query_rows, key_rows, query, window, soft, grad_attended,
    grad_query_rows, grad_pair, grad_carry, first_carry, projections_keep, projections_send,
    turned, grad_window, both_rows, query_sum, pair_sum,
):
    step = pl.program_id(0)
    steps = pl.num_programs(0)
    width = query.shape[1]

    @pl.when(step == 0)
    def _():
        query_sum[...] = jnp.zeros_like(query_sum)
        pair_sum[...] = jnp.zeros_like(pair_sum)

    for p in range(PARTS):
        pulled = dot(pick_query[...], grad_attended[p * PART_ROWS : (p + 1) * PART_ROWS]).astype(BF)
        for g in range(PART // GROUP):
            tile = p * (PART // GROUP) + g
            rows = slice(tile * TILE, (tile + 1) * TILE)
            spread = slice(g * TILE, (g + 1) * TILE)
            for h in range(PAIRS):
                lanes = slice(h * PAIR, (h + 1) * PAIR)
                value_lanes = slice(width + h * PAIR, width + (h + 1) * PAIR)
                keys = window[rows, lanes]
                values = window[rows, value_lanes]
                asks = two_heads(query[rows, lanes])
                grads = two_heads(pulled[spread, lanes])
                spot = (tile * PAIRS + h) * TILE
                soft_low = soft[spot : spot + TILE]
                soft_wide = soft_low.astype(F32)
                weighted = dot_back(values, grads) * soft_wide
                grad_scores = (weighted - soft_wide * jnp.sum(weighted, axis=0, keepdims=True)).astype(BF)
                grad_window[spread, lanes] = dot(grad_scores, asks).astype(BF)
                grad_window[spread, value_lanes] = dot(soft_low, grads).astype(BF)
                turned[lanes, spread] = of_two_heads(dot_outer(keys, grad_scores))
        part = slice(p * PART_ROWS, (p + 1) * PART_ROWS)
        grad_asks = dot_back(unpick_query[...], turned[...]).astype(BF)
        grad_query_rows[part] = grad_asks
        both = dot(unpick_key[...], grad_window[...]).astype(BF)
        grad_pair[part] = both[:PART_ROWS]
        grad_carry[p * CARRY : (p + 1) * CARRY] = both[PART_ROWS:]
        if p == 0:
            store_first(first_carry, both[PART_ROWS:], step)
        both_rows[p * (PART_ROWS + CARRY) : (p + 1) * (PART_ROWS + CARRY)] = both
    query_sum[...] += dot_outer(query_rows[...], grad_query_rows[...])
    pair_sum[...] += dot_outer(key_rows[...], both_rows[...])

    @pl.when(step == steps - 1)
    def _():
        for half, out in ((core[0], projections_keep), (1 - core[0], projections_send)):
            rows = pl.ds(pl.multiple_of(half * (width // 2), width // 2), width // 2)
            out[:, :width] = (query_sum[rows] * 0.125).astype(BF)
            out[:, width:] = pair_sum[rows].astype(BF)


def projection_back_kernel(
    unpick_carry, grad_pair, grad_carry, carry_next, grad_query_rows, frames, grad_residual, query_w, key_w, value_w, gain,
    grad_frames, grad_memory, grad_gain,
):
    step = pl.program_id(0)
    steps = pl.num_programs(0)
    width = query_w.shape[0]
    pairs = []
    for p in range(PARTS):
        after = step * PARTS + p + 1
        inside = jnp.minimum(after, steps * PARTS - 1)
        late = grad_carry[pl.ds(pl.multiple_of(inside * CARRY, CARRY), CARRY)]
        if p == PARTS - 1:
            late = jnp.where(step == steps - 1, carry_next[...].astype(F32), late.astype(F32)).astype(BF)
        pairs.append(grad_pair[p * PART_ROWS : (p + 1) * PART_ROWS].astype(F32) + dot(unpick_carry[...], late))
    pair = jnp.concatenate(pairs, axis=0).astype(BF)
    query_back = dot_back(grad_query_rows[...], query_w[...]) * 0.125
    key_back = dot_back(pair[:, :width], key_w[...]) + dot_back(pair[:, width:], value_w[...])
    memory_rows, results = [], []
    gain_part = jnp.zeros((1, width), F32)
    for p, part in enumerate(by_part(frames[...].astype(F32))):
        at = p * PART_ROWS
        end = at + PART_FRAMES
        memory_rows.append(key_back[end : end + PART])
        own = query_back[at:end] + key_back[at:end]
        share = query_back[end : end + PART] * (1.0 / SEGLEN)
        share = jnp.concatenate([jnp.zeros((RIGHT * PART, width), F32)] + [share] * SEGLEN, axis=0)
        unit, scale = row_stats(part)
        grad_norm, more = norm_back(unit, scale, gain[...], own + share)
        gain_part = gain_part + more
        results.append(grad_residual[p * PART_FRAMES : (p + 1) * PART_FRAMES].astype(F32) + grad_norm)
    grad_frames[...] = by_frame(results)
    grad_memory[...] = jnp.concatenate(memory_rows, axis=0).astype(BF)

    @pl.when(step == 0)
    def _():
        grad_gain[...] = gain_part

    @pl.when(step > 0)
    def _():
        grad_gain[...] += gain_part


def cost(us):
    return pl.CostEstimate(flops=int(us * 1e9), bytes_accessed=int(us * 1e5), transcendentals=0)


def segment_position(counts_row, segment):
    order = jnp.arange(counts_row.shape[0], dtype=jnp.int32)
    starts = jnp.sum(jnp.where(order[None, :] < order[:, None], counts_row[None, :], 0), axis=1)
    first = jnp.max(jnp.where(starts[None, :] <= segment[:, None], starts[None, :], 0), axis=1)
    return segment - first


def shift(values, axis, by):
    size = lax.axis_size(axis)
    return lax.ppermute(values, axis, [(i, (i + by) % size) for i in range(size)])


def axis_bits(axis):
    return [1 << i for i in range(lax.axis_size(axis).bit_length() - 1)]


def chain(turn):
    bits = axis_bits("seg")
    few = min(3, len(bits))

    def turned(by):
        by = by % max(1, few)
        return bits[by:few] + bits[:by] + bits[few:]

    return ["grp"] + list(zip(turned(turn), turned(turn + 1)))


def side(stage):
    if stage == "grp":
        return lax.axis_index("grp")
    place = lax.axis_index("seg")
    return jnp.where(lax.axis_index("grp") == 0, place // stage[0] % 2, place // stage[1] % 2)


def swap(values, stage):
    if stage == "grp":
        return lax.ppermute(values, "grp", [(0, 1), (1, 0)])
    size = lax.axis_size("seg")
    pairs = [(core * size + i, core * size + (i ^ stage[core])) for core in range(2) for i in range(size)]
    return lax.ppermute(values, ("grp", "seg"), pairs)


def split_sum(total):
    high = total.astype(BF)
    return high, (total - high.astype(F32)).astype(BF)


class Sum:
    def __init__(self, keep, send, turn):
        self.values = keep
        self.first = send
        self.turn = turn
        self.steps = chain(turn)
        self.done = 0
        self.row = None

    def start(self, tie=None):
        count = len(self.steps)
        if self.done < count:
            stage = self.steps[self.done]
            if self.done == 0:
                send = self.first
            else:
                rows = self.values.shape[0] // 2
                own = side(stage)
                self.values, send = (
                    lax.dynamic_slice_in_dim(self.values, half * rows, rows, 0) for half in (own, 1 - own)
                )
        else:
            stage = self.steps[2 * count - 1 - self.done]
            send = self.values
            if self.row is not None:
                blank = jnp.zeros((6, self.row.shape[1]), BF)
                send = jnp.concatenate([send, *split_sum(self.row), blank], axis=0)
        if tie is not None:
            send, _ = lax.optimization_barrier((send, tie))
        self.arriving = swap(send, stage)
        return send

    def land(self, *ties):
        count = len(self.steps)
        other = lax.optimization_barrier((self.arriving,) + ties)[0] if ties else self.arriving
        if self.done < count:
            self.values = (self.values.astype(F32) + other.astype(F32)).astype(self.values.dtype)
        else:
            rows = self.values.shape[0]
            if self.row is not None:
                high, low = split_sum(self.row)
                theirs = other[rows : rows + 1].astype(F32) + other[rows + 1 : rows + 2].astype(F32)
                self.row = high.astype(F32) + low.astype(F32) + theirs
                other = other[:rows]
            if self.done < 2 * count - 1:
                self.values = jnp.concatenate([self.values, other], axis=0)
            else:
                self.other = other
        self.done += 1

    def complete(self):
        return self.done == 2 * len(self.steps)


def shares(turn, core, place):
    found = []
    for which in range(2):
        share = 0
        for stage in chain(turn)[1:]:
            share = share * 2 + place // stage[which] % 2
        found.append(share)
    return jnp.where(core == 0, found[0], found[1]), jnp.where(core == 0, found[1], found[0])


def finish(total, widths, device):
    own, other = total.values, total.other
    half = own.shape[0]
    count = lax.axis_size("seg")
    rows = half // count
    cuts = np.cumsum(widths)[:-1].tolist()
    if rows % 16:
        index = jnp.arange(count, dtype=jnp.int32)
        mine, theirs = (
            jnp.take(part.reshape(count, rows, -1), index ^ share, axis=0).reshape(half, -1)
            for part, share in zip((own, other[:half]), shares(total.turn, device[0], device[1]))
        )
        whole = jnp.where(device[0] == 0, jnp.concatenate([mine, theirs]), jnp.concatenate([theirs, mine]))
        return jnp.split(whole.astype(F32), cuts, axis=1)
    halves = 2

    def kernel(device_ref, own_ref, other_ref, *outs):
        step = pl.program_id(0)
        mine = (step // halves) == device_ref[0]
        own_share, other_share = shares(total.turn, device_ref[0], device_ref[1])

        def fill(source, share):
            for j in range(count // halves):
                piece = (step % halves * (count // halves) + j) ^ share
                block = source[pl.ds(pl.multiple_of(piece * rows, rows), rows)].astype(F32)
                at = 0
                for out in outs:
                    out[j * rows : (j + 1) * rows] = block[:, at : at + out.shape[1]]
                    at += out.shape[1]

        @pl.when(mine)
        def _():
            fill(own_ref, own_share)

        @pl.when(jnp.logical_not(mine))
        def _():
            fill(other_ref, other_share)

    return pl.pallas_call(
        kernel,
        grid=(2 * halves,),
        in_specs=[pl.BlockSpec(memory_space=pltpu.SMEM)] + [pl.BlockSpec(part.shape, lambda i: (0, 0)) for part in (own, other)],
        out_specs=[pl.BlockSpec((half // halves, w), lambda i: (i, 0)) for w in widths],
        out_shape=[jax.ShapeDtypeStruct((2 * half, w), F32) for w in widths],
        compiler_params=pltpu.CompilerParams(vmem_limit_bytes=FINISH_VMEM),
        cost_estimate=cost(3),
        name="finish",
    )(device, own, other)


def call(kernel, steps, operands, outs, scratch, us, aliases=None):
    def spec(shape, block):
        if isinstance(block, pl.BlockSpec):
            return block
        if block is None:
            return pl.BlockSpec(shape, lambda i: (0,) * len(shape))
        if len(block) == 3:
            return pl.BlockSpec(block, lambda i: (0, i, 0))
        return pl.BlockSpec(block, lambda i: (i, 0))

    return pl.pallas_call(
        kernel,
        grid=(steps,),
        in_specs=[spec(array.shape, block) for array, block in operands],
        out_specs=[spec(shape, block) for _, shape, block in outs],
        out_shape=[jax.ShapeDtypeStruct(shape, dtype) for dtype, shape, _ in outs],
        scratch_shapes=[pltpu.VMEM(shape, dtype) for dtype, shape in scratch],
        input_output_aliases=aliases or {},
        compiler_params=pltpu.CompilerParams(vmem_limit_bytes=VMEM_LIMIT),
        cost_estimate=cost(us),
        name=kernel.__name__,
    )(*[array for array, _ in operands])


def per_device(
    frames_in, memory, counts, query_weight, key_weight, value_weight, out_weight, up_weight, down_weight,
    input_gain, middle_gain, output_gain, out_grad, memory_grad,
):
    slots, _, width = frames_in.shape
    ff = up_weight.shape[1]
    steps = slots // BLOCK
    total = slots * FRAMES
    parts = slots // PART
    tiles = slots // GROUP
    pick_query, pick_key, pick_carry, need, segment_of = tables()
    unpick_query, unpick_key, unpick_carry = (jnp.asarray(pick.T, BF) for pick in (pick_query, pick_key, pick_carry))
    pick_late = jnp.asarray(pick_key[:, PART_ROWS:], BF)
    pick_query, pick_key, pick_carry = (jnp.asarray(pick, BF) for pick in (pick_query, pick_key, pick_carry))
    device = jnp.stack([lax.axis_index("grp"), lax.axis_index("seg")]).astype(jnp.int32)
    need, segment_of = jnp.asarray(need), jnp.asarray(segment_of)
    input_gain, middle_gain, output_gain = (g.reshape(1, width) for g in (input_gain, middle_gain, output_gain))
    frames = jnp.transpose(frames_in, (1, 0, 2))
    pulls = jnp.transpose(out_grad, (1, 0, 2))
    segment = lax.axis_index("seg") * slots + jnp.arange(slots, dtype=jnp.int32)
    position = segment_position(counts[0], segment)
    halo = jnp.concatenate([frames[:, slots - PART :], memory[None, slots - PART :]], axis=0)
    halo = shift(halo, "seg", 1)
    slab = (FRAMES, BLOCK, width)
    smem = pl.BlockSpec(memory_space=pltpu.SMEM)

    query_rows, key_rows, query, window = call(
        project_kernel,
        steps,
        [
            (frames, slab), (memory, (BLOCK, width)), (input_gain, None),
            (query_weight, None), (key_weight, None), (value_weight, None),
            (pick_query, None), (pick_key, None), (pick_carry, None),
        ],
        [
            (BF, (parts * PART_ROWS, width), (FULL, width)),
            (BF, (parts * (PART_ROWS + CARRY), width), (PARTS * (PART_ROWS + CARRY), width)),
            (BF, (tiles * TILE, width), (TILES, width)),
            (BF, (tiles * TILE, 2 * width), (TILES, 2 * width)),
        ],
        [(BF, (CARRY, width)), (BF, (CARRY, 2 * width))],
        10,
    )

    key_block = pl.BlockSpec((PART_ROWS + CARRY, width), lambda i: (0, 0))
    window_block = pl.BlockSpec((PART_TILES, 2 * width), lambda i: (0, 0))
    key_rows, window = call(
        halo_kernel,
        1,
        [
            (halo, pl.BlockSpec(halo.shape, lambda i: (0, 0, 0))), (input_gain, None), (key_weight, None), (value_weight, None),
            (pick_carry, None), (pick_late, None),
            (key_rows, key_block), (window, window_block),
        ],
        [(BF, key_rows.shape, key_block), (BF, window.shape, window_block)],
        [],
        2,
        {6: 0, 7: 1},
    )

    attended, soft, residual, slope, grad_combined, result, memory_out, keep, send, output_part = call(
        forward_kernel,
        steps,
        [
            (device, smem), (position, smem), (need, None), (segment_of, None), (unpick_query, None),
            (query, (TILES, width)), (window, (TILES, 2 * width)), (frames, slab), (pulls, slab),
            (middle_gain, None), (output_gain, None), (out_weight, None), (up_weight, None), (down_weight, None),
        ],
        [
            (BF, (parts * PART_ROWS, width), (FULL, width)),
            (BF, (tiles * PAIRS * TILE, 2 * TILE), (TILES * PAIRS, 2 * TILE)),
            (BF, (total, width), (ROWS, width)),
            (BF, (total, ff), (ROWS, ff)),
            (BF, (total, width), (ROWS, width)),
            (BF, (FRAMES, slots, width), slab),
            (BF, (slots, width), (BLOCK, width)),
            (BF, (ff // 2, width), None),
            (BF, (ff // 2, width), None),
            (F32, (1, width), None),
        ],
        [(BF, (width, PART_TILES)), (BF, (total, ff)), (BF, (total, width))],
        24,
    )

    down = Sum(keep, send, 0)
    down.start()

    grad_residual, grad_attended, keep, send, middle_part = call(
        backward_kernel,
        steps,
        [
            (device, smem), (slope, (ROWS, ff)), (grad_combined, (ROWS, width)), (residual, (ROWS, width)), (attended, (FULL, width)),
            (memory_grad, (BLOCK, width)), (middle_gain, None), (out_weight, None), (up_weight, None), (down_weight, None),
        ],
        [
            (BF, (total, width), (ROWS, width)),
            (BF, (parts * PART_ROWS, width), (FULL, width)),
            (BF, (width // 2, ff + width), None),
            (BF, (width // 2, ff + width), None),
            (F32, (1, width), None),
        ],
        [(BF, (total, ff)), (BF, (total, width)), (F32, (width, width))],
        16,
    )

    down.land()
    down.values, grad_attended = lax.optimization_barrier((down.values, grad_attended))
    up = Sum(keep, send, 1)
    up.start()
    down.start()

    grad_query_rows, grad_pair, grad_carry, first_carry, keep, send = call(
        attention_back_kernel,
        steps,
        [
            (device, smem), (pick_query, None), (unpick_query, None), (unpick_key, None),
            (query_rows, (FULL, width)), (key_rows, (PARTS * (PART_ROWS + CARRY), width)),
            (query, (TILES, width)), (window, (TILES, 2 * width)),
            (soft, (TILES * PAIRS, 2 * TILE)), (grad_attended, (FULL, width)),
        ],
        [
            (BF, (parts * PART_ROWS, width), (FULL, width)),
            (BF, (parts * PART_ROWS, 2 * width), (FULL, 2 * width)),
            (BF, (parts * CARRY, 2 * width), (PARTS * CARRY, 2 * width)),
            (BF, (CARRY, 2 * width), None),
            (BF, (width // 2, 3 * width), None),
            (BF, (width // 2, 3 * width), None),
        ],
        [
            (BF, (width, PART_TILES)), (BF, (PART_TILES, 2 * width)), (BF, (PARTS * (PART_ROWS + CARRY), 2 * width)),
            (F32, (width, width)), (F32, (width, 2 * width)),
        ],
        12,
    )

    projections = Sum(keep, send, 2)
    sent = projections.start()
    carry_next = shift(first_carry, "seg", -1)
    down.land()
    up.land()
    down.values, up.values, grad_pair = lax.optimization_barrier((down.values, up.values, grad_pair))
    sent = up.start(sent)
    sent = down.start(sent)
    projections.land(sent)
    sent = projections.start(sent)
    grad_pair, _ = lax.optimization_barrier((grad_pair, sent))

    grad_frames, grad_memory, input_part = call(
        projection_back_kernel,
        steps,
        [
            (unpick_carry, None), (grad_pair, (FULL, 2 * width)), (grad_carry, None), (carry_next, None),
            (grad_query_rows, (FULL, width)), (frames, slab), (grad_residual, (ROWS, width)),
            (query_weight, None), (key_weight, None), (value_weight, None), (input_gain, None),
        ],
        [
            (F32, (FRAMES, slots, width), slab),
            (BF, (slots, width), (BLOCK, width)),
            (F32, (1, width), None),
        ],
        [],
        8,
    )
    result = jnp.transpose(result, (1, 0, 2))
    grad_frames = jnp.transpose(grad_frames, (1, 0, 2))

    gains = jnp.concatenate([input_part, middle_part, output_part], axis=1)
    up.land(sent, gains)
    projections.row = None
    order = (up, down, projections)
    cuts = {up: [ff, width], down: [width], projections: [width] * 3}
    ready = {}
    held = ()
    turn = 0
    while not all(one.complete() for one in order):
        one = order[turn % 3]
        turn += 1
        if one.complete():
            continue
        if turn > 1:
            one.land(sent, *(held if one is projections else ()))
        if one is projections and one.done == len(one.steps):
            one.row = gains
        if one.complete():
            ready[one] = finish(one, cuts[one], device)
            held = held + tuple(ready[one])
        else:
            sent = one.start(sent)
    gains = projections.row
    (grad_down,) = ready[down]
    grad_up, grad_out = ready[up]
    grad_query, grad_key, grad_value = ready[projections]
    gains = gains.reshape(3, width)
    return (
        result, memory_out, grad_frames, grad_memory,
        grad_query, grad_key, grad_value, grad_out, grad_up, grad_down,
        gains[0], gains[1], gains[2],
    )


def solution(mesh):
    rows = P(("grp", "seg"), None, None)
    singles = P(("grp", "seg"), None)
    return jax.shard_map(
        per_device,
        mesh=mesh,
        in_specs=(rows, singles, P("grp", None)) + (P(),) * 9 + (rows, singles),
        out_specs=(rows, singles, rows, singles) + (P(),) * 9,
        check_vma=False,
    )
```
